128 devices in a mesh: item: 64 (over z, y, x_hi, core), qgrp: 2 (over x_lo).
Axes of the slice: x: 4 (x_hi: 2, x_lo: 2; x = x_hi * 2 + x_lo), y: 4, z: 4, core: 2. Of those that a mesh axis runs over, the one named last changes fastest.
Arguments:
- hidden: bfloat16 [131072, 3584], P(('item', 'qgrp')), may hold values from -6 to 6
- w_query: bfloat16 [3584, 1024], P(('item', 'qgrp')), may hold values from -0.09375 to 0.09375
- adapter: bfloat16 [1024, 1024], replicated, may hold values from -0.1875 to 0.1875
- item_emb: bfloat16 [2048, 1024], P(('item', 'qgrp')), may hold values from -120 to 120
- counts: int32 [2048], replicated, may hold values from 256 to 4095
- positive: int32 [131072], P(('item', 'qgrp')), may hold values from 0 to 2047
- loss_weight: float32 [131072], P(('item', 'qgrp')), may hold values from 0.02 to 0.1
Outputs:
- grad_query_weight: float32 [3584, 1024], P(('item', 'qgrp'))
- grad_adapter: float32 [1024, 1024], P(('item', 'qgrp'))
- loss: float32 [], replicated
The draws below stay inside these ranges and needn't reach their ends.
All inputs are finite; a program needn't handle non-finite values.
Results may differ from the reference program's by a relative error of at most 0.0047.
Values may be sent and summed in bfloat16 or wider, within the bound.
A program may use at most 128 MiB of HBM per device.

```python
import math
import jax
import jax.numpy as jnp
from jax import lax

H = 3584
E = 1024
QUERIES = 131072
NEG = 2048


def draw_item_emb(key, part):
    key = jax.random.fold_in(key, 11)
    base_key, scale_key = jax.random.split(key, 2)
    row_scale = jnp.exp(jax.random.uniform(scale_key, (NEG, 1), jnp.float32, -0.25, -0.05))
    values = jax.random.truncated_normal(base_key, -4.0, 4.0, (NEG, E), jnp.float32) * row_scale
    return values.astype(jnp.bfloat16)


def with_ends(values, rng, low, largest):
    dims = values.shape
    spot = [jax.random.randint(jax.random.fold_in(rng, axis), (), 0, dims[axis]) for axis in range(len(dims))]
    values = values.at[tuple(spot)].set(low)
    longest = dims.index(max(dims))
    spot[longest] = (spot[longest] + 1) % dims[longest]
    return values.at[tuple(spot)].set(largest)


def level_of(own_key, shape, cuts, smallest, largest):
    gain = 1.0
    for dim, blocks in cuts:
        steps = jax.random.uniform(jax.random.fold_in(jax.random.fold_in(own_key, 6), dim), (blocks,), jnp.float32, smallest / len(cuts), largest / len(cuts))
        gain = gain * jnp.repeat(jnp.exp(steps), shape[dim] // blocks).reshape((-1,) + (1,) * (len(shape) - 1 - dim))
    return gain


def bell_draw(stream_key, dims, width, reach, shards=(), kind=jnp.bfloat16):
    result = width * jax.random.normal(stream_key, dims, jnp.float32)
    if shards:
        result = result * level_of(stream_key, dims, shards, -0.22, 0.18)
    return jnp.clip(result, -reach, reach).astype(kind)


def setup_inputs(seed: int = 0) -> dict:
    key_list = jax.random.split(jax.random.key(seed), 8)
    return {
        "hidden": bell_draw(key_list[0], (QUERIES, H), 1.0, 6.0, ((0, 128),)),
        "w_query": bell_draw(key_list[1], (H, E), H ** -0.5, 0.09375, ((0, 128),)),
        "adapter": bell_draw(key_list[2], (E, E), E ** -0.5, 0.1875),
        "item_emb": draw_item_emb(jax.random.fold_in(key_list[7], 71), 0),
        "counts": with_ends(jax.random.randint(key_list[4], (NEG,), 256, 4096), jax.random.fold_in(key_list[4], 1), 256, 4095).astype(jnp.int32),
        "positive": with_ends(jax.random.randint(key_list[5], (QUERIES,), 0, NEG), jax.random.fold_in(key_list[5], 1), 0, NEG - 1).astype(jnp.int32),
        "loss_weight": jnp.clip(0.02 + 0.08 * jax.random.uniform(key_list[6], (QUERIES,), jnp.float32) ** level_of(key_list[6], (QUERIES,), ((0, 128),), -0.2, 0.2), 0.02, 0.1),
    }


def reference(hidden, w_query, adapter, item_emb, counts, positive, loss_weight):
    scale = 2.0 / math.sqrt(E)
    adapted = (item_emb.astype(jnp.float32) + jnp.dot(item_emb, adapter, preferred_element_type=jnp.float32)).astype(jnp.bfloat16)
    log_count = jnp.log(counts.astype(jnp.float32))
    block = math.gcd(QUERIES, 4096)
    turns = QUERIES // block

    def one_block(carry, index):
        grad_query, grad_items, total = carry
        start = (index * block).astype(jnp.int32)
        rows = lax.dynamic_slice_in_dim(hidden, start, block, 0)
        targets = lax.dynamic_slice_in_dim(positive, start, block, 0)
        weights = lax.dynamic_slice_in_dim(loss_weight, start, block, 0)
        queries = jnp.dot(rows, w_query, preferred_element_type=jnp.float32).astype(jnp.bfloat16)
        logits = scale * jnp.dot(queries, adapted.T, preferred_element_type=jnp.float32) - log_count[None, :]
        top = lax.optimization_barrier(jnp.max(logits, axis=1, keepdims=True))
        shifted = jnp.exp(logits - top)
        denom = lax.optimization_barrier(jnp.sum(shifted, axis=1, keepdims=True))
        onehot = (jnp.arange(NEG, dtype=jnp.int32)[None, :] == targets[:, None]).astype(jnp.float32)
        picked = lax.optimization_barrier(jnp.sum(logits * onehot, axis=1))
        losses = jnp.log(denom[:, 0]) + top[:, 0] - picked
        coeff = (weights[:, None] * (shifted / denom - onehot)).astype(jnp.bfloat16)
        grad_q = (scale * jnp.dot(coeff, adapted, preferred_element_type=jnp.float32)).astype(jnp.bfloat16)
        grad_items = grad_items + scale * jnp.dot(coeff.T, queries, preferred_element_type=jnp.float32)
        grad_query = grad_query + jnp.dot(rows.T, grad_q, preferred_element_type=jnp.float32)
        total = total + jnp.sum(weights * losses)
        return ((grad_query, grad_items, total), None)
    init = (jnp.zeros((H, E), jnp.float32), jnp.zeros((NEG, E), jnp.float32), jnp.zeros((), jnp.float32))
    (grad_query, grad_items, total), _ = lax.scan(one_block, init, jnp.arange(turns, dtype=jnp.int32))
    grad_adapter = jnp.dot(item_emb.astype(jnp.float32).T, grad_items, precision=lax.Precision.HIGHEST)
    return (grad_query, grad_adapter, total / QUERIES)
```

```python
import functools
import math

import jax
import jax.numpy as jnp
from jax import lax
from jax.experimental import pallas as pl
from jax.experimental.pallas import tpu as pltpu
from jax.sharding import PartitionSpec as P

MESH = pl.DeviceIdType.MESH
F32, BF16 = jnp.float32, jnp.bfloat16
AXES = ("item", "qgrp")
LINE = 8
SIDE = 4
QUARTERS, WIDE = 4, 256
ROWS = 256


def dot(a, b, contract=(1, 0)):
    dims = (((contract[0],), (contract[1],)), ((), ()))
    return lax.dot_general(a, b, dims, preferred_element_type=F32)


def place():
    item, low = lax.axis_index("item"), lax.axis_index("qgrp")
    return item // 16, (item // 4) % 4, (item // 2) % 2, item % 2, low


def device(z, y, high, core, low):
    return (z * 16 + y * 4 + high * 2 + core, low)


def select(shape, source):
    row = lax.broadcasted_iota(jnp.int32, shape, 0)
    col = lax.broadcasted_iota(jnp.int32, shape, 1)
    return jnp.where(col == source(row), 1.0, 0.0).astype(BF16)


def step_kernel(
    scale, hidden_ref, w_ref, adapter_ref, item_ref, counts_ref, positive_ref, weight_ref,
    gw_ref, ga_ref, loss_ref,
    hid, hid_t, ada, wall, xs, pool, adapted, queries, grad_q, pulled, pos_col, weight_col, log_count,
    sib_in, first_z, first_y, second_in, slot_out, slot_in, loss_out, loss_in,
    load_sem, xs_s, xs_r, w_s, w_r, ws_s, ws_r, e_s, e_r, sib_s, sib_r, fz_s, fz_r, fy_s, fy_r, se_s, se_r,
    sl_s, sl_r, lo_s, lo_r,
):
    z, y, high, core, low = place()
    slot = high * 4 + core * 2 + low
    block_rows = LINE * w_ref.shape[0]
    own_rows = w_ref.shape[0]
    adapter_rows = ga_ref.shape[0]
    group = SIDE * block_rows
    sibling = device(z, y, high, 1 - core, low)

    def z_peer(o):
        return device((z + o) % SIDE, y, high, core, low)

    def y_peer(o):
        return device(z, (y + o) % SIDE, high, core, low)

    def flip(k):
        return (high + k // 4) % 2, (core + (k // 2) % 2) % 2, (low + k % 2) % 2

    def line_peer(k):
        h, c, l = flip(k)
        return device(z, y, h, c, l)

    def line_slot(k):
        h, c, l = flip(k)
        return h * 4 + c * 2 + l

    def remote(src, dst, send, recv, to):
        return pltpu.make_async_remote_copy(
            src_ref=src, dst_ref=dst, send_sem=send, recv_sem=recv, device_id=to, device_id_type=MESH
        )

    loads = [
        pltpu.make_async_copy(hidden_ref.at[:, pl.ds(group * k, group)], hid.at[k], load_sem.at[k])
        for k in range(SIDE)
    ]
    loads.append(pltpu.make_async_copy(adapter_ref, ada, load_sem.at[SIDE]))
    for load in loads:
        load.start()

    barrier = pltpu.get_barrier_semaphore()
    peers = [line_peer(k) for k in range(1, LINE)]
    peers += [z_peer(o) for o in (1, 2, 3)] + [y_peer(o) for o in (1, 2, 3)]
    for peer in peers:
        pl.semaphore_signal(barrier, inc=1, device_id=peer, device_id_type=MESH)

    xs[slot, :, own_rows:, :] = jnp.zeros((QUARTERS, 32 - own_rows, WIDE), BF16)
    for q in range(QUARTERS):
        xs[slot, q, 0:own_rows, :] = w_ref[:, q * WIDE:(q + 1) * WIDE]
    pool[z, y, slot] = item_ref[...]
    pl.semaphore_wait(barrier, len(peers))

    sent = []

    def send(copy):
        copy.start()
        sent.append(copy)

    for k in (2, 1, 3, 4, 6, 5, 7):
        pair = pl.ds(2 * flip(k)[1], 2)
        send(remote(xs.at[slot, pair], xs.at[slot, pair], xs_s.at[k], xs_r.at[k], line_peer(k)))
    own_e = pool.at[z, y, slot]
    for o in (1, 2, 3):
        send(remote(own_e, own_e, e_s.at[o - 1], e_r.at[o - 1], z_peer(o)))

    log_count[...] = jnp.log(counts_ref[...].astype(F32))
    for r in range(positive_ref.shape[0]):
        rows = pl.ds(r * 128, 128)
        line = positive_ref[r:r + 1, :].astype(F32)
        pos_col[rows, :] = jnp.broadcast_to(line, (128, 128)).T
        weight_col[rows, :] = jnp.broadcast_to(weight_ref[r:r + 1, :], (128, 128)).T

    for o in (1, 2, 3):
        got = pool.at[(z - o + SIDE) % SIDE, y, slot]
        remote(got, got, e_s.at[o - 1], e_r.at[o - 1], z_peer(o)).wait_recv()
    column_e = pool.at[:, y, slot]
    for o in (1, 2, 3):
        send(remote(column_e, column_e, e_s.at[2 + o], e_r.at[2 + o], y_peer(o)))

    for k in range(1, LINE):
        got = xs.at[line_slot(k), pl.ds(2 * core, 2)]
        remote(got, got, xs_s.at[k], xs_r.at[k], line_peer(k)).wait_recv()
    half = 4 * own_rows

    def source(row):
        skipped = sum(jnp.where(row >= own_rows * s, 32 - own_rows, 0) for s in (1, 2, 3))
        return row + skipped

    pick = select((half, 128), source)
    here = z * SIDE + y
    for p in range(2):
        q = 2 * core + p
        for h in range(2):
            padded = jnp.reshape(xs[4 * h:4 * h + 4, q], (128, WIDE))
            wall[q, here, half * h:half * (h + 1), :] = dot(pick, padded).astype(BF16)

    def w_block(p, of, og):
        if p == 0:
            b = ((z - og + SIDE) % SIDE) * SIDE + (y - of + SIDE) % SIDE
        else:
            b = ((z - of + SIDE) % SIDE) * SIDE + (y - og + SIDE) % SIDE
        return b

    def w_at(p, of, og, c=None):
        q = 2 * (core if c is None else c) + p
        return wall.at[q, w_block(p, of, og), pl.ds(0, block_rows)]

    def w_send(p, of, og, new_of, new_og, to):
        at = w_at(p, of, og)
        n = new_of * SIDE + new_og
        send(remote(at, at, w_s.at[p, n], w_r.at[p, n], to))

    def w_wait(p, of, og):
        at = w_at(p, of, og)
        n = of * SIDE + og
        remote(at, at, w_s.at[p, n], w_r.at[p, n], sibling).wait_recv()

    def w_share(p, of, og):
        at = w_at(p, of, og)
        n = of * SIDE + og
        send(remote(at, at, ws_s.at[p, n], ws_r.at[p, n], sibling))

    near = ((y_peer, z_peer), (z_peer, y_peer))
    for o in (1, 3, 2):
        for p in range(2):
            w_send(p, 0, 0, o, 0, near[p][0](o))
    for o in (1, 3, 2):
        for p in range(2):
            w_send(p, 0, 0, 0, o, near[p][1](o))
    for p in range(2):
        w_share(p, 0, 0)

    for o in (1, 2, 3):
        got = pool.at[:, (y - o + SIDE) % SIDE, slot]
        remote(got, got, e_s.at[2 + o], e_r.at[2 + o], y_peer(o)).wait_recv()
    slab = pool.at[:, :, slot]
    for n, k in enumerate((1, 4, 5)):
        send(remote(slab, slab, e_s.at[6 + n], e_r.at[6 + n], line_peer(k)))
    send(remote(slab, slab, e_s.at[9], e_r.at[9], sibling))

    for of in (1, 3, 2):
        for p in range(2):
            w_wait(p, of, 0)
            for og in (1, 3, 2):
                w_send(p, of, 0, of, og, near[p][1](og))
            w_share(p, of, 0)

    for k in range(SIDE):
        loads[k].wait()
        for s in range(group // 128):
            hid_t[k, 128 * s:128 * (s + 1), :] = hid[k, :, 128 * s:128 * (s + 1)].T
        if k == 1:
            for p in range(2):
                for og in (1, 3, 2):
                    w_wait(p, 0, og)
                    w_share(p, 0, og)
    for n, k in enumerate((1, 4, 5)):
        got = pool.at[:, :, line_slot(k)]
        remote(got, got, e_s.at[6 + n], e_r.at[6 + n], line_peer(k)).wait_recv()
        send(remote(got, got, e_s.at[10 + n], e_r.at[10 + n], sibling))
    for p in range(2):
        for of in (1, 3, 2):
            for og in (1, 3, 2):
                w_wait(p, of, og)
                w_share(p, of, og)
    for n, k in enumerate((2, 3, 6, 7)):
        got = pool.at[:, :, line_slot(k)]
        remote(got, got, e_s.at[9 + n], e_r.at[9 + n], sibling).wait_recv()

    loads[SIDE].wait()
    chunk = pool.shape[2] * pool.shape[3] * 2

    def adapt(i, carry):
        rows = pl.ds(pl.multiple_of(i * chunk, chunk), chunk)
        items = jnp.reshape(pool[i // 2, pl.ds((i % 2) * 2, 2)], (chunk, pool.shape[4]))
        adapted[rows, :] = (items.astype(F32) + dot(items, ada[...])).astype(BF16)
        return carry

    lax.fori_loop(0, adapted.shape[0] // chunk, adapt, 0)

    for p in range(2):
        for of in range(SIDE):
            for og in range(SIDE):
                at = w_at(p, of, og, 1 - core)
                n = of * SIDE + og
                remote(at, at, ws_s.at[p, n], ws_r.at[p, n], sibling).wait_recv()

    def project(i, carry):
        cols = pl.ds(pl.multiple_of(i * WIDE, WIDE), WIDE)
        total = None
        for k in range(SIDE):
            part = jnp.reshape(wall[i, SIDE * k:SIDE * (k + 1), 0:block_rows, :], (group, WIDE))
            term = dot(hid[k], part)
            total = term if total is None else total + term
        queries[:, cols] = total.astype(BF16)
        return carry

    lax.fori_loop(0, QUARTERS, project, 0)

    items_all = adapted.shape[0]

    def softmax(i, total):
        rows = pl.ds(pl.multiple_of(i * ROWS, ROWS), ROWS)
        logits = scale * dot(queries[rows, :], adapted[...], (1, 1)) - log_count[...]
        top = jnp.max(logits, axis=1, keepdims=True)
        shifted = jnp.exp(logits - top)
        denom = jnp.sum(shifted, axis=1, keepdims=True)
        lane = lax.broadcasted_iota(jnp.int32, (ROWS, items_all), 1).astype(F32)
        hit = lane == pos_col[rows, 0:1]
        picked = jnp.sum(jnp.where(hit, logits, 0.0), axis=1, keepdims=True)
        weight = weight_col[rows, 0:1]
        losses = jnp.log(denom) + top - picked
        plain = shifted * (weight / denom)
        coeff = jnp.where(hit, plain - weight, plain).astype(BF16)
        grad_q[rows, :] = (scale * dot(coeff, adapted[...])).astype(BF16)
        items = jnp.reshape(pool[...], (items_all, pool.shape[4]))
        pulled[rows, :] = dot(coeff, items).astype(BF16)
        return total + jnp.sum(weight * losses)

    total = lax.fori_loop(0, queries.shape[0] // ROWS, softmax, jnp.zeros((), F32))

    def loss_send(stage, n, to):
        send(remote(loss_out.at[stage], loss_in.at[stage, n], lo_s.at[stage, n], lo_r.at[stage, n], to))

    def loss_sum(stage, count):
        value = loss_out[stage]
        for n in range(count):
            remote(
                loss_out.at[stage], loss_in.at[stage, n], lo_s.at[stage, n], lo_r.at[stage, n], sibling
            ).wait_recv()
            value = value + loss_in[stage, n]
        return value

    loss_out[0] = jnp.full((8, 128), total, F32)
    loss_send(0, 0, sibling)

    for copy in sent[:-1]:
        copy.wait_send()
    del sent[:-1]

    full = wall.shape[2]

    def unit(k, q):
        cols = pl.ds(pl.multiple_of(q * WIDE, WIDE), WIDE)
        upper = dot(hid_t[k], grad_q[:, cols])
        span = full - block_rows
        taken = pulled[:, pl.ds(pl.multiple_of(k * SIDE * span, SIDE * span), SIDE * span)]
        lower = dot(taken, queries[:, cols], (0, 0))
        return jnp.reshape(upper, (SIDE, block_rows, WIDE)), jnp.reshape(lower, (SIDE, span, WIDE))

    def sib_copy(p, k, c):
        four = pl.ds(k * SIDE, SIDE)
        return remote(
            wall.at[2 * c + p, four], sib_in.at[p, four], sib_s.at[p, k], sib_r.at[p, k], sibling
        )

    def fz_copy(o):
        four = pl.ds(((z + o) % SIDE) * SIDE, SIDE)
        return remote(wall.at[2 * core, four], first_z.at[o - 1], fz_s.at[o - 1], fz_r.at[o - 1], z_peer(o))

    def fy_copy(k, o):
        b = k * SIDE + (y + o) % SIDE
        n = o - 1
        return remote(wall.at[2 * core + 1, b], first_y.at[n, k], fy_s.at[n, k], fy_r.at[n, k], y_peer(o))

    def reduce_group(i, carry):
        k = (z + 1 + i) % SIDE
        four = pl.ds(k * SIDE, SIDE)
        for p in range(2):
            q = 2 * (1 - core) + p
            upper, lower = unit(k, q)
            wall[q, four, 0:block_rows, :] = upper.astype(BF16)
            wall[q, four, block_rows:full, :] = lower.astype(BF16)
            sib_copy(p, k, 1 - core).start()
        for p in range(2):
            q = 2 * core + p
            upper, lower = unit(k, q)
            sib_copy(p, k, 1 - core).wait_recv()
            wall[q, four, 0:block_rows, :] = (upper + sib_in[p, four, 0:block_rows, :].astype(F32)).astype(BF16)
            wall[q, four, block_rows:full, :] = (lower + sib_in[p, four, block_rows:full, :].astype(F32)).astype(BF16)
            if p == 0:
                @pl.when(i < SIDE - 1)
                def _():
                    b = pl.ds(k * SIDE, SIDE)
                    remote(
                        wall.at[2 * core, b], first_z.at[i], fz_s.at[i], fz_r.at[i],
                        device(k, y, high, core, low),
                    ).start()
            else:
                for o in (1, 2, 3):
                    fy_copy(k, o).start()
        return carry

    lax.fori_loop(0, SIDE, reduce_group, 0)

    loss_out[1] = loss_sum(0, 1)
    for o in (1, 2, 3):
        loss_send(1, o - 1, z_peer(o))

    def second_copy(p, o):
        if p == 0:
            b, to = z * SIDE + (y + o) % SIDE, y_peer(o)
        else:
            b, to = ((z + o) % SIDE) * SIDE + y, z_peer(o)
        return remote(
            wall.at[2 * core + p, b], second_in.at[p, o - 1], se_s.at[p, o - 1], se_r.at[p, o - 1], to
        )

    mine = [None, None]
    for o in (1, 2, 3):
        fz_copy(o).wait_recv()
    for o in (1, 2, 3, 0):
        yy = (y + o) % SIDE
        value = wall[2 * core, z * SIDE + yy].astype(F32)
        for n in range(3):
            value = value + first_z[n, yy].astype(F32)
        if o:
            wall[2 * core, z * SIDE + yy] = value.astype(BF16)
            second_copy(0, o).start()
        else:
            mine[0] = value
    for o in (1, 2, 3, 0):
        zz = (z + o) % SIDE
        b = zz * SIDE + y
        value = wall[2 * core + 1, b].astype(F32)
        for n in range(3):
            fy_copy(zz, n + 1).wait_recv()
            value = value + first_y[n, zz].astype(F32)
        if o:
            wall[2 * core + 1, b] = value.astype(BF16)
            second_copy(1, o).start()
        else:
            mine[1] = value

    loss_out[2] = loss_sum(1, 3)
    for o in (1, 2, 3):
        loss_send(2, o - 1, y_peer(o))

    tall = slot_out.shape[2]
    shape = (LINE * tall, full)
    row = lax.broadcasted_iota(jnp.int32, shape, 0)
    col = lax.broadcasted_iota(jnp.int32, shape, 1)
    owner = sum(jnp.where(row >= tall * s, 1, 0) for s in range(1, LINE))
    inner = row - tall * owner
    from_w = (inner < own_rows) & (col == own_rows * owner + inner)
    from_a = (inner >= 32) & (inner < 32 + adapter_rows) & (col == block_rows + adapter_rows * owner + inner - 32)
    spread = jnp.where(from_w | from_a, 1.0, 0.0).astype(BF16)
    for p in range(2):
        value = mine[p]
        for o in (1, 2, 3):
            second_copy(p, o).wait_recv()
            value = value + second_in[p, o - 1].astype(F32)
        slots = dot(spread, value.astype(BF16)).astype(BF16)
        slot_out[p] = jnp.reshape(slots, (LINE, tall, WIDE))

    def slot_copy(k):
        return remote(
            slot_out.at[:, line_slot(k)], slot_in.at[k], sl_s.at[k], sl_r.at[k], line_peer(k)
        )

    for k in (1, 4, 5, 3, 6, 7, 2):
        slot_copy(k).start()

    loss_out[3] = loss_sum(2, 3)
    for n, k in enumerate((1, 4, 5)):
        loss_send(3, n, line_peer(k))

    for k in range(1, LINE):
        slot_copy(k).wait_recv()
    for p in range(2):
        same = slot_out[p, slot].astype(F32)
        for k in (1, 4, 5):
            same = same + slot_in[k, p].astype(F32)
        other = slot_in[2, p].astype(F32)
        for k in (3, 6, 7):
            other = other + slot_in[k, p].astype(F32)
        for value, c in ((same, core), (other, 1 - core)):
            cols = pl.ds(pl.multiple_of((2 * c + p) * WIDE, WIDE), WIDE)
            gw_ref[:, cols] = value[0:own_rows]
            ga_ref[:, cols] = scale * value[32:32 + adapter_rows]

    loss_ref[...] = loss_sum(3, 3)

    for copy in sent:
        copy.wait_send()
    for p in range(2):
        for k in range(SIDE):
            sib_copy(p, k, 1 - core).wait_send()
    for o in (1, 2, 3):
        fz_copy(o).wait_send()
        for k in range(SIDE):
            fy_copy(k, o).wait_send()
        for p in range(2):
            second_copy(p, o).wait_send()
    for k in range(1, LINE):
        slot_copy(k).wait_send()


def on_device(hidden, w_query, adapter, item_emb, counts, positive, loss_weight):
    scale = 2.0 / math.sqrt(adapter.shape[0])
    devices = lax.axis_size(AXES)
    queries, deep = hidden.shape
    wide = adapter.shape[0]
    items = counts.shape[0]
    block = LINE * w_query.shape[0]
    full = block + LINE * (wide // devices)
    sem = pltpu.SemaphoreType.DMA
    vmem = pl.BlockSpec(memory_space=pltpu.VMEM)
    anywhere = pl.BlockSpec(memory_space=pl.ANY)
    gw, ga, loss = pl.pallas_call(
        functools.partial(step_kernel, scale),
        out_shape=(
            jax.ShapeDtypeStruct((w_query.shape[0], wide), F32),
            jax.ShapeDtypeStruct((wide // devices, wide), F32),
            jax.ShapeDtypeStruct((8, 128), F32),
        ),
        in_specs=[anywhere, vmem, anywhere, vmem, vmem, vmem, vmem],
        out_specs=(vmem, vmem, vmem),
        scratch_shapes=[
            pltpu.VMEM((SIDE, queries, deep // SIDE), BF16),
            pltpu.VMEM((SIDE, deep // SIDE, queries), BF16),
            pltpu.VMEM((wide, wide), BF16),
            pltpu.VMEM((QUARTERS, 16, full, WIDE), BF16),
            pltpu.VMEM((LINE, QUARTERS, 32, WIDE), BF16),
            pltpu.VMEM((SIDE, SIDE, LINE, items // devices, wide), BF16),
            pltpu.VMEM((items, wide), BF16),
            pltpu.VMEM((queries, wide), BF16),
            pltpu.VMEM((queries, wide), BF16),
            pltpu.VMEM((queries, wide), BF16),
            pltpu.VMEM((queries, 128), F32),
            pltpu.VMEM((queries, 128), F32),
            pltpu.VMEM((1, items), F32),
            pltpu.VMEM((2, 16, full, WIDE), BF16),
            pltpu.VMEM((3, SIDE, full, WIDE), BF16),
            pltpu.VMEM((3, SIDE, full, WIDE), BF16),
            pltpu.VMEM((2, 3, full, WIDE), BF16),
            pltpu.VMEM((2, LINE, 48, WIDE), BF16),
            pltpu.VMEM((LINE, 2, 48, WIDE), BF16),
            pltpu.VMEM((4, 8, 128), F32),
            pltpu.VMEM((4, 3, 8, 128), F32),
            sem((SIDE + 1,)),
            sem((LINE,)), sem((LINE,)),
            sem((2, 16)), sem((2, 16)),
            sem((2, 16)), sem((2, 16)),
            sem((13,)), sem((13,)),
            sem((2, SIDE)), sem((2, SIDE)),
            sem((3,)), sem((3,)),
            sem((3, SIDE)), sem((3, SIDE)),
            sem((2, 3)), sem((2, 3)),
            sem((LINE,)), sem((LINE,)),
            sem((4, 3)), sem((4, 3)),
        ],
        compiler_params=pltpu.CompilerParams(
            collective_id=0, has_side_effects=True, vmem_limit_bytes=64 * 1024 * 1024 - 65536
        ),
        name="sampled_softmax_step",
    )(
        hidden, w_query, adapter, item_emb, counts.reshape(1, items),
        positive.reshape(queries // 128, 128), loss_weight.reshape(queries // 128, 128),
    )
    return gw, ga, loss[0, 0] / (queries * devices)


def solution(mesh):
    placed = (P(AXES, None), P(AXES, None), P(), P(AXES, None), P(), P(AXES), P(AXES))
    return jax.shard_map(
        on_device,
        mesh=mesh,
        in_specs=placed,
        out_specs=(P(AXES, None), P(AXES, None), P()),
        check_vma=False,
    )
```

```python
import functools
import math

import jax
import jax.numpy as jnp
from jax import lax
from jax.experimental import pallas as pl
from jax.experimental.pallas import tpu as pltpu
from jax.sharding import PartitionSpec as P

MESH = pl.DeviceIdType.MESH
F32, BF16 = jnp.float32, jnp.bfloat16
AXES = ("item", "qgrp")
LINE = 8
SIDE = 4
QUARTERS, WIDE = 4, 256
ROWS = 256


def dot(a, b, contract=(1, 0)):
    dims = (((contract[0],), (contract[1],)), ((), ()))
    return lax.dot_general(a, b, dims, preferred_element_type=F32)


def place():
    item, low = lax.axis_index("item"), lax.axis_index("qgrp")
    return item // 16, (item // 4) % 4, (item // 2) % 2, item % 2, low


def device(z, y, high, core, low):
    return (z * 16 + y * 4 + high * 2 + core, low)


def select(shape, source):
    row = lax.broadcasted_iota(jnp.int32, shape, 0)
    col = lax.broadcasted_iota(jnp.int32, shape, 1)
    return jnp.where(col == source(row), 1.0, 0.0).astype(BF16)


def step_kernel(
    scale, hidden_ref, w_ref, adapter_ref, item_ref, counts_ref, positive_ref, weight_ref,
    gw_ref, ga_ref, loss_ref,
    hid, hid_t, ada, wall, xs, pool, adapted, partial, queries, coeff, grad_q, pulled, pos_col, weight_col, log_count,
    sib_in, first_z, first_y, second_in, slot_out, slot_in, loss_out, loss_in,
    load_sem, xs_s, xs_r, w_s, w_r, ws_s, ws_r, ez_s, ez_r, ey_s, ey_r, ex_s, ex_r, es_s, es_r, sib_s, sib_r, fz_s, fz_r, fy_s, fy_r, se_s, se_r,
    sl_s, sl_r, lo_s, lo_r,
):
    z, y, high, core, low = place()
    slot = high * 4 + core * 2 + low
    block_rows = LINE * w_ref.shape[0]
    own_rows = w_ref.shape[0]
    adapter_rows = ga_ref.shape[0]
    group = SIDE * block_rows
    sibling = device(z, y, high, 1 - core, low)

    def z_peer(o):
        return device((z + o) % SIDE, y, high, core, low)

    def x_peer(o):
        xx = (2 * high + low + o) % SIDE
        return device(z, y, xx // 2, core, xx % 2)

    def y_peer(o):
        return device(z, (y + o) % SIDE, high, core, low)

    def flip(k):
        return (high + k // 4) % 2, (core + (k // 2) % 2) % 2, (low + k % 2) % 2

    def line_peer(k):
        h, c, l = flip(k)
        return device(z, y, h, c, l)

    def line_slot(k):
        h, c, l = flip(k)
        return h * 4 + c * 2 + l

    def remote(src, dst, send, recv, to):
        return pltpu.make_async_remote_copy(
            src_ref=src, dst_ref=dst, send_sem=send, recv_sem=recv, device_id=to, device_id_type=MESH
        )

    loads = [
        pltpu.make_async_copy(hidden_ref.at[:, pl.ds(group * k, group)], hid.at[k], load_sem.at[k])
        for k in range(SIDE)
    ]
    loads.append(pltpu.make_async_copy(adapter_ref, ada, load_sem.at[SIDE]))
    for load in loads:
        load.start()

    barrier = pltpu.get_barrier_semaphore()
    peers = [line_peer(k) for k in range(1, LINE)]
    peers += [z_peer(o) for o in (1, 2, 3)] + [y_peer(o) for o in (1, 2, 3)]
    for peer in peers:
        pl.semaphore_signal(barrier, inc=1, device_id=peer, device_id_type=MESH)

    xs[slot, :, own_rows:, :] = jnp.zeros((QUARTERS, 32 - own_rows, WIDE), BF16)
    for q in range(QUARTERS):
        xs[slot, q, 0:own_rows, :] = w_ref[:, q * WIDE:(q + 1) * WIDE]
    pool[z, y, slot] = item_ref[...]
    pl.semaphore_wait(barrier, len(peers))

    sent = []

    def send(copy):
        copy.start()
        sent.append(copy)

    for k in (2, 1, 3, 4, 6, 5, 7):
        pair = pl.ds(2 * flip(k)[1], 2)
        send(remote(xs.at[slot, pair], xs.at[slot, pair], xs_s.at[k], xs_r.at[k], line_peer(k)))
    own_e = pool.at[z, y, slot]
    for o in (1, 2, 3):
        send(remote(own_e, own_e, ez_s.at[o - 1], ez_r.at[o - 1], z_peer(o)))

    log_count[...] = jnp.log(counts_ref[...].astype(F32))
    for r in range(positive_ref.shape[0]):
        rows = pl.ds(r * 128, 128)
        line = positive_ref[r:r + 1, :].astype(F32)
        pos_col[rows, :] = jnp.broadcast_to(line, (128, 128)).T
        weight_col[rows, :] = jnp.broadcast_to(weight_ref[r:r + 1, :], (128, 128)).T

    def e_column(o, ox, c):
        xx = (2 * high + low - ox + SIDE) % SIDE
        return pool.at[:, (y - o + SIDE) % SIDE, (xx // 2) * 4 + c * 2 + xx % 2]

    def e_along(o, ox, new_ox, to):
        at = e_column(o, ox, core)
        send(remote(at, at, ex_s.at[new_ox - 1, o], ex_r.at[new_ox - 1, o], x_peer(to)))

    def e_share(o, ox):
        at = e_column(o, ox, core)
        send(remote(at, at, es_s.at[ox, o], es_r.at[ox, o], sibling))

    def e_wait_x(o, ox):
        at = e_column(o, ox, core)
        remote(at, at, ex_s.at[ox - 1, o], ex_r.at[ox - 1, o], sibling).wait_recv()

    for o in (1, 2, 3):
        got = pool.at[(z - o + SIDE) % SIDE, y, slot]
        remote(got, got, ez_s.at[o - 1], ez_r.at[o - 1], z_peer(o)).wait_recv()
    own_column = e_column(0, 0, core)
    for o in (1, 3, 2):
        send(remote(own_column, own_column, ey_s.at[o - 1], ey_r.at[o - 1], y_peer(o)))
    for o in (1, 3):
        e_along(0, 0, o, o)

    for k in range(1, LINE):
        got = xs.at[line_slot(k), pl.ds(2 * core, 2)]
        remote(got, got, xs_s.at[k], xs_r.at[k], line_peer(k)).wait_recv()
    half = 4 * own_rows

    def source(row):
        skipped = sum(jnp.where(row >= own_rows * s, 32 - own_rows, 0) for s in (1, 2, 3))
        return row + skipped

    pick = select((half, 128), source)
    here = z * SIDE + y
    for p in range(2):
        q = 2 * core + p
        for h in range(2):
            padded = jnp.reshape(xs[4 * h:4 * h + 4, q], (128, WIDE))
            wall[q, here, half * h:half * (h + 1), :] = dot(pick, padded).astype(BF16)

    def w_block(p, of, og):
        if p == 0:
            b = ((z - og + SIDE) % SIDE) * SIDE + (y - of + SIDE) % SIDE
        else:
            b = ((z - of + SIDE) % SIDE) * SIDE + (y - og + SIDE) % SIDE
        return b

    def w_at(p, of, og, c=None):
        q = 2 * (core if c is None else c) + p
        return wall.at[q, w_block(p, of, og), pl.ds(0, block_rows)]

    def w_send(p, of, og, new_of, new_og, to):
        at = w_at(p, of, og)
        n = new_of * SIDE + new_og
        send(remote(at, at, w_s.at[p, n], w_r.at[p, n], to))

    def w_wait(p, of, og):
        at = w_at(p, of, og)
        n = of * SIDE + og
        remote(at, at, w_s.at[p, n], w_r.at[p, n], sibling).wait_recv()

    def w_share(p, of, og):
        at = w_at(p, of, og)
        n = of * SIDE + og
        send(remote(at, at, ws_s.at[p, n], ws_r.at[p, n], sibling))

    near = ((y_peer, z_peer), (z_peer, y_peer))
    for o in (1, 3, 2):
        for p in range(2):
            w_send(p, 0, 0, o, 0, near[p][0](o))
    for o in (1, 3):
        for p in range(2):
            w_send(p, 0, 0, 0, o, near[p][1](o))
    for p in range(2):
        w_share(p, 0, 0)
    e_share(0, 0)

    def transpose(k):
        loads[k].wait()
        for s in range(group // 128):
            hid_t[k, 128 * s:128 * (s + 1), :] = hid[k, :, 128 * s:128 * (s + 1)].T

    transpose(0)
    for o in (1, 3, 2):
        got = e_column(o, 0, core)
        remote(got, got, ey_s.at[o - 1], ey_r.at[o - 1], y_peer(o)).wait_recv()
        for ox in (1, 3):
            e_along(o, 0, ox, ox)
        e_share(o, 0)
    for of in (1, 3, 2):
        for p in range(2):
            w_wait(p, of, 0)
            for og in (1, 3):
                w_send(p, of, 0, of, og, near[p][1](og))
            w_share(p, of, 0)
    transpose(1)

    for n, o in enumerate((0, 1, 3, 2)):
        for ox in (1, 3):
            e_wait_x(o, ox)
            if ox == (1 if n < 2 else 3):
                e_along(o, ox, 2, 1 if ox == 1 else 3)
            e_share(o, ox)
        for p in range(2):
            for og in (1, 3):
                w_wait(p, o, og)
                if og == (1 if n < 2 else 3):
                    w_send(p, o, og, o, 2, near[p][1](og))
                w_share(p, o, og)
        if n < 2:
            transpose(2 + n)

    def w_got(p, of, og):
        at = w_at(p, of, og, 1 - core)
        n = of * SIDE + og
        remote(at, at, ws_s.at[p, n], ws_r.at[p, n], sibling).wait_recv()

    def project(q, offset):
        k = (z - offset + SIDE) % SIDE
        part = jnp.reshape(wall[q, pl.ds(SIDE * k, SIDE), 0:block_rows, :], (group, WIDE))
        return dot(hid[k], part)

    own_first, sib_first = 2 * core, 2 * (1 - core)
    partial[0] = project(own_first, 0) + project(own_first, 1) + project(own_first, 3)
    for of in (0, 1, 3, 2):
        for og in (0, 1, 3):
            w_got(0, of, og)
    partial[1] = project(sib_first, 0) + project(sib_first, 1) + project(sib_first, 3)

    for o in (0, 1, 3, 2):
        e_wait_x(o, 2)
        e_share(o, 2)
        for p in range(2):
            w_wait(p, o, 2)
            w_share(p, o, 2)
    for ox in range(SIDE):
        for o in range(SIDE):
            got = e_column(o, ox, 1 - core)
            remote(got, got, es_s.at[ox, o], es_r.at[ox, o], sibling).wait_recv()

    loads[SIDE].wait()
    chunk = pool.shape[2] * pool.shape[3] * 2

    def adapt(i, carry):
        rows = pl.ds(pl.multiple_of(i * chunk, chunk), chunk)
        items = jnp.reshape(pool[i // 2, pl.ds((i % 2) * 2, 2)], (chunk, pool.shape[4]))
        adapted[rows, :] = (items.astype(F32) + dot(items, ada[...])).astype(BF16)
        return carry

    lax.fori_loop(0, adapted.shape[0] // chunk, adapt, 0)

    def columns(q):
        return pl.ds(pl.multiple_of(q * WIDE, WIDE), WIDE)

    queries[:, columns(own_first)] = (partial[0] + project(own_first, 2)).astype(BF16)
    own_next = sum(project(own_first + 1, o) for o in range(SIDE))
    queries[:, columns(own_first + 1)] = own_next.astype(BF16)
    for of in range(SIDE):
        w_got(0, of, 2)
    queries[:, columns(sib_first)] = (partial[1] + project(sib_first, 2)).astype(BF16)
    for of in range(SIDE):
        for og in range(SIDE):
            w_got(1, of, og)
    sib_next = sum(project(sib_first + 1, o) for o in range(SIDE))
    queries[:, columns(sib_first + 1)] = sib_next.astype(BF16)

    items_all = adapted.shape[0]

    def softmax(i, total):
        rows = pl.ds(pl.multiple_of(i * ROWS, ROWS), ROWS)
        logits = scale * dot(queries[rows, :], adapted[...], (1, 1)) - log_count[...]
        top = jnp.max(logits, axis=1, keepdims=True)
        shifted = jnp.exp(logits - top)
        denom = jnp.sum(shifted, axis=1, keepdims=True)
        lane = lax.broadcasted_iota(jnp.int32, (ROWS, items_all), 1).astype(F32)
        hit = lane == pos_col[rows, 0:1]
        picked = jnp.sum(jnp.where(hit, logits, 0.0), axis=1, keepdims=True)
        weight = weight_col[rows, 0:1]
        losses = jnp.log(denom) + top - picked
        plain = shifted * (weight / denom)
        part = jnp.where(hit, plain - weight, plain).astype(BF16)
        coeff[rows, :] = part
        grad_q[rows, :] = (scale * dot(part, adapted[...])).astype(BF16)
        return total + jnp.sum(weight * losses)

    total = lax.fori_loop(0, queries.shape[0] // ROWS, softmax, jnp.zeros((), F32))

    def loss_send(stage, n, to):
        send(remote(loss_out.at[stage], loss_in.at[stage, n], lo_s.at[stage, n], lo_r.at[stage, n], to))

    def loss_sum(stage, count):
        value = loss_out[stage]
        for n in range(count):
            remote(
                loss_out.at[stage], loss_in.at[stage, n], lo_s.at[stage, n], lo_r.at[stage, n], sibling
            ).wait_recv()
            value = value + loss_in[stage, n]
        return value

    loss_out[0] = jnp.full((8, 128), total, F32)
    loss_send(0, 0, sibling)

    for copy in sent[:-1]:
        copy.wait_send()
    del sent[:-1]

    full = wall.shape[2]
    span = full - block_rows

    def unit(k, q):
        cols = columns(q)
        upper = dot(hid_t[k], grad_q[:, cols])
        lower = dot(pulled[...], queries[:, cols])
        return jnp.reshape(upper, (SIDE, block_rows, WIDE)), jnp.reshape(lower, (SIDE, span, WIDE))

    def sib_copy(p, k, c):
        four = pl.ds(k * SIDE, SIDE)
        return remote(
            wall.at[2 * c + p, four], sib_in.at[p, four], sib_s.at[p, k], sib_r.at[p, k], sibling
        )

    def fz_copy(o):
        four = pl.ds(((z + o) % SIDE) * SIDE, SIDE)
        return remote(wall.at[2 * core, four], first_z.at[o - 1], fz_s.at[o - 1], fz_r.at[o - 1], z_peer(o))

    def fy_copy(k, o):
        b = k * SIDE + (y + o) % SIDE
        n = o - 1
        return remote(wall.at[2 * core + 1, b], first_y.at[n, k], fy_s.at[n, k], fy_r.at[n, k], y_peer(o))

    def reduce_group(i, carry):
        k = (z + 1 + i) % SIDE
        four = pl.ds(k * SIDE, SIDE)
        some = pool[:, :, :, :, pl.ds(pl.multiple_of(k * SIDE * span, SIDE * span), SIDE * span)]
        pulled[...] = dot(coeff[...], jnp.reshape(some, (items_all, SIDE * span))).T.astype(BF16)
        for p in range(2):
            q = 2 * (1 - core) + p
            upper, lower = unit(k, q)
            wall[q, four, 0:block_rows, :] = upper.astype(BF16)
            wall[q, four, block_rows:full, :] = lower.astype(BF16)
            sib_copy(p, k, 1 - core).start()
        for p in range(2):
            q = 2 * core + p
            upper, lower = unit(k, q)
            sib_copy(p, k, 1 - core).wait_recv()
            wall[q, four, 0:block_rows, :] = (upper + sib_in[p, four, 0:block_rows, :].astype(F32)).astype(BF16)
            wall[q, four, block_rows:full, :] = (lower + sib_in[p, four, block_rows:full, :].astype(F32)).astype(BF16)
            if p == 0:
                @pl.when(i < SIDE - 1)
                def _():
                    b = pl.ds(k * SIDE, SIDE)
                    remote(
                        wall.at[2 * core, b], first_z.at[i], fz_s.at[i], fz_r.at[i],
                        device(k, y, high, core, low),
                    ).start()
            else:
                for o in (1, 2, 3):
                    fy_copy(k, o).start()
        return carry

    lax.fori_loop(0, SIDE, reduce_group, 0)

    loss_out[1] = loss_sum(0, 1)
    for o in (1, 2, 3):
        loss_send(1, o - 1, z_peer(o))

    def second_copy(p, o):
        if p == 0:
            b, to = z * SIDE + (y + o) % SIDE, y_peer(o)
        else:
            b, to = ((z + o) % SIDE) * SIDE + y, z_peer(o)
        return remote(
            wall.at[2 * core + p, b], second_in.at[p, o - 1], se_s.at[p, o - 1], se_r.at[p, o - 1], to
        )

    mine = [None, None]
    for o in (1, 2, 3):
        fz_copy(o).wait_recv()
    for o in (1, 2, 3, 0):
        yy = (y + o) % SIDE
        value = wall[2 * core, z * SIDE + yy].astype(F32)
        for n in range(3):
            value = value + first_z[n, yy].astype(F32)
        if o:
            wall[2 * core, z * SIDE + yy] = value.astype(BF16)
            second_copy(0, o).start()
        else:
            mine[0] = value
    for o in (1, 2, 3, 0):
        zz = (z + o) % SIDE
        b = zz * SIDE + y
        value = wall[2 * core + 1, b].astype(F32)
        for n in range(3):
            fy_copy(zz, n + 1).wait_recv()
            value = value + first_y[n, zz].astype(F32)
        if o:
            wall[2 * core + 1, b] = value.astype(BF16)
            second_copy(1, o).start()
        else:
            mine[1] = value

    loss_out[2] = loss_sum(1, 3)
    for o in (1, 2, 3):
        loss_send(2, o - 1, y_peer(o))

    tall = slot_out.shape[2]
    shape = (LINE * tall, full)
    row = lax.broadcasted_iota(jnp.int32, shape, 0)
    col = lax.broadcasted_iota(jnp.int32, shape, 1)
    owner = sum(jnp.where(row >= tall * s, 1, 0) for s in range(1, LINE))
    inner = row - tall * owner
    from_w = (inner < own_rows) & (col == own_rows * owner + inner)
    from_a = (inner >= 32) & (inner < 32 + adapter_rows) & (col == block_rows + adapter_rows * owner + inner - 32)
    spread = jnp.where(from_w | from_a, 1.0, 0.0).astype(BF16)
    for p in range(2):
        value = mine[p]
        for o in (1, 2, 3):
            second_copy(p, o).wait_recv()
            value = value + second_in[p, o - 1].astype(F32)
        slots = dot(spread, value.astype(BF16)).astype(BF16)
        slot_out[p] = jnp.reshape(slots, (LINE, tall, WIDE))

    def slot_copy(k):
        return remote(
            slot_out.at[:, line_slot(k)], slot_in.at[k], sl_s.at[k], sl_r.at[k], line_peer(k)
        )

    for k in (1, 4, 5, 3, 6, 7, 2):
        slot_copy(k).start()

    loss_out[3] = loss_sum(2, 3)
    for n, k in enumerate((1, 4, 5)):
        loss_send(3, n, line_peer(k))

    for k in range(1, LINE):
        slot_copy(k).wait_recv()
    for p in range(2):
        same = slot_out[p, slot].astype(F32)
        for k in (1, 4, 5):
            same = same + slot_in[k, p].astype(F32)
        other = slot_in[2, p].astype(F32)
        for k in (3, 6, 7):
            other = other + slot_in[k, p].astype(F32)
        for value, c in ((same, core), (other, 1 - core)):
            cols = pl.ds(pl.multiple_of((2 * c + p) * WIDE, WIDE), WIDE)
            gw_ref[:, cols] = value[0:own_rows]
            ga_ref[:, cols] = scale * value[32:32 + adapter_rows]

    loss_ref[...] = loss_sum(3, 3)

    for copy in sent:
        copy.wait_send()
    for p in range(2):
        for k in range(SIDE):
            sib_copy(p, k, 1 - core).wait_send()
    for o in (1, 2, 3):
        fz_copy(o).wait_send()
        for k in range(SIDE):
            fy_copy(k, o).wait_send()
        for p in range(2):
            second_copy(p, o).wait_send()
    for k in range(1, LINE):
        slot_copy(k).wait_send()


def finish_kernel(share, gw_in, ga_in, loss_in, gw_ref, ga_ref, loss_ref):
    gw_ref[...] = gw_in[...]
    ga_ref[...] = ga_in[...]
    loss_ref[...] = loss_in[0:1, 0:1] * share


def on_device(hidden, w_query, adapter, item_emb, counts, positive, loss_weight):
    scale = 2.0 / math.sqrt(adapter.shape[0])
    devices = lax.axis_size(AXES)
    queries, deep = hidden.shape
    wide = adapter.shape[0]
    items = counts.shape[0]
    block = LINE * w_query.shape[0]
    full = block + LINE * (wide // devices)
    sem = pltpu.SemaphoreType.DMA
    vmem = pl.BlockSpec(memory_space=pltpu.VMEM)
    anywhere = pl.BlockSpec(memory_space=pl.ANY)
    gw, ga, loss = pl.pallas_call(
        functools.partial(step_kernel, scale),
        out_shape=(
            jax.ShapeDtypeStruct((w_query.shape[0], wide), F32),
            jax.ShapeDtypeStruct((wide // devices, wide), F32),
            jax.ShapeDtypeStruct((8, 128), F32),
        ),
        in_specs=[anywhere, vmem, anywhere, vmem, vmem, vmem, vmem],
        out_specs=(vmem, vmem, vmem),
        scratch_shapes=[
            pltpu.VMEM((SIDE, queries, deep // SIDE), BF16),
            pltpu.VMEM((SIDE, deep // SIDE, queries), BF16),
            pltpu.VMEM((wide, wide), BF16),
            pltpu.VMEM((QUARTERS, 16, full, WIDE), BF16),
            pltpu.VMEM((LINE, QUARTERS, 32, WIDE), BF16),
            pltpu.VMEM((SIDE, SIDE, LINE, items // devices, wide), BF16),
            pltpu.VMEM((items, wide), BF16),
            pltpu.VMEM((2, queries, WIDE), F32),
            pltpu.VMEM((queries, wide), BF16),
            pltpu.VMEM((queries, items), BF16),
            pltpu.VMEM((queries, wide), BF16),
            pltpu.VMEM((wide // SIDE, queries), BF16),
            pltpu.VMEM((queries, 128), F32),
            pltpu.VMEM((queries, 128), F32),
            pltpu.VMEM((1, items), F32),
            pltpu.VMEM((2, 16, full, WIDE), BF16),
            pltpu.VMEM((3, SIDE, full, WIDE), BF16),
            pltpu.VMEM((3, SIDE, full, WIDE), BF16),
            pltpu.VMEM((2, 3, full, WIDE), BF16),
            pltpu.VMEM((2, LINE, 48, WIDE), BF16),
            pltpu.VMEM((LINE, 2, 48, WIDE), BF16),
            pltpu.VMEM((4, 8, 128), F32),
            pltpu.VMEM((4, 3, 8, 128), F32),
            sem((SIDE + 1,)),
            sem((LINE,)), sem((LINE,)),
            sem((2, 16)), sem((2, 16)),
            sem((2, 16)), sem((2, 16)),
            sem((3,)), sem((3,)),
            sem((3,)), sem((3,)),
            sem((3, SIDE)), sem((3, SIDE)),
            sem((SIDE, SIDE)), sem((SIDE, SIDE)),
            sem((2, SIDE)), sem((2, SIDE)),
            sem((3,)), sem((3,)),
            sem((3, SIDE)), sem((3, SIDE)),
            sem((2, 3)), sem((2, 3)),
            sem((LINE,)), sem((LINE,)),
            sem((4, 3)), sem((4, 3)),
        ],
        compiler_params=pltpu.CompilerParams(
            collective_id=0, has_side_effects=True, vmem_limit_bytes=64 * 1024 * 1024 - 65536
        ),
        name="sampled_softmax_step",
    )(
        hidden, w_query, adapter, item_emb, counts.reshape(1, items),
        positive.reshape(queries // 128, 128), loss_weight.reshape(queries // 128, 128),
    )
    gw, ga, loss = pl.pallas_call(
        functools.partial(finish_kernel, 1.0 / (queries * devices)),
        out_shape=(
            jax.ShapeDtypeStruct(gw.shape, F32),
            jax.ShapeDtypeStruct(ga.shape, F32),
            jax.ShapeDtypeStruct((1, 1), F32),
        ),
        in_specs=[vmem, vmem, vmem],
        out_specs=(vmem, vmem, vmem),
        name="finish",
    )(gw, ga, loss)
    return gw, ga, loss.reshape(())


def solution(mesh):
    placed = (P(AXES, None), P(AXES, None), P(), P(AXES, None), P(), P(AXES), P(AXES))
    return jax.shard_map(
        on_device,
        mesh=mesh,
        in_specs=placed,
        out_specs=(P(AXES, None), P(AXES, None), P()),
        check_vma=False,
    )
```

```python
import functools
import math

import jax
import jax.numpy as jnp
from jax import lax
from jax.experimental import pallas as pl
from jax.experimental.pallas import tpu as pltpu
from jax.sharding import PartitionSpec as P

MESH = pl.DeviceIdType.MESH
F32, BF16 = jnp.float32, jnp.bfloat16
AXES = ("item", "qgrp")
LINE = 8
SIDE = 4
QUARTERS, WIDE = 4, 256
ROWS = 256


def dot(a, b, contract=(1, 0)):
    dims = (((contract[0],), (contract[1],)), ((), ()))
    return lax.dot_general(a, b, dims, preferred_element_type=F32)


def place():
    item, low = lax.axis_index("item"), lax.axis_index("qgrp")
    return item // 16, (item // 4) % 4, (item // 2) % 2, item % 2, low


def device(z, y, high, core, low):
    return (z * 16 + y * 4 + high * 2 + core, low)


def select(shape, source):
    row = lax.broadcasted_iota(jnp.int32, shape, 0)
    col = lax.broadcasted_iota(jnp.int32, shape, 1)
    return jnp.where(col == source(row), 1.0, 0.0).astype(BF16)


def step_kernel(
    scale, hidden_ref, w_ref, adapter_ref, item_ref, counts_ref, positive_ref, weight_ref,
    gw_ref, ga_ref, loss_ref,
    hid, hid_t, wall, xs, pool, adapted, partial, queries, coeff, grad_q, pulled, pos_col, weight_col, log_count,
    sib_in, first_z, first_y, second_in, slot_out, slot_in, loss_out, loss_in,
    load_sem, xs_s, xs_r, w_s, w_r, ws_s, ws_r, ez_s, ez_r, ey_s, ey_r, ex_s, ex_r, es_s, es_r, sib_s, sib_r, fz_s, fz_r, fy_s, fy_r, se_s, se_r,
    sl_s, sl_r, lo_s, lo_r,
):
    z, y, high, core, low = place()
    slot = high * 4 + core * 2 + low
    block_rows = LINE * w_ref.shape[0]
    own_rows = w_ref.shape[0]
    adapter_rows = ga_ref.shape[0]
    group = SIDE * block_rows
    sibling = device(z, y, high, 1 - core, low)

    def z_peer(o):
        return device((z + o) % SIDE, y, high, core, low)

    def x_peer(o):
        xx = (2 * high + low + o) % SIDE
        return device(z, y, xx // 2, core, xx % 2)

    def y_peer(o):
        return device(z, (y + o) % SIDE, high, core, low)

    def flip(k):
        return (high + k // 4) % 2, (core + (k // 2) % 2) % 2, (low + k % 2) % 2

    def line_peer(k):
        h, c, l = flip(k)
        return device(z, y, h, c, l)

    def line_slot(k):
        h, c, l = flip(k)
        return h * 4 + c * 2 + l

    def remote(src, dst, send, recv, to):
        return pltpu.make_async_remote_copy(
            src_ref=src, dst_ref=dst, send_sem=send, recv_sem=recv, device_id=to, device_id_type=MESH
        )

    loads = [
        pltpu.make_async_copy(
            hidden_ref.at[:, pl.ds(group * k, group)], coeff.at[:, pl.ds(group * (k % 2), group)], load_sem.at[k]
        )
        for k in range(SIDE)
    ]
    loads.append(pltpu.make_async_copy(adapter_ref, grad_q, load_sem.at[SIDE]))
    for k in (0, 1, SIDE):
        loads[k].start()

    barrier = pltpu.get_barrier_semaphore()
    peers = [line_peer(k) for k in range(1, LINE)]
    peers += [z_peer(o) for o in (1, 2, 3)] + [y_peer(o) for o in (1, 2, 3)]
    for peer in peers:
        pl.semaphore_signal(barrier, inc=1, device_id=peer, device_id_type=MESH)

    xs[slot, :, own_rows:, :] = jnp.zeros((QUARTERS, 32 - own_rows, WIDE), BF16)
    for q in range(QUARTERS):
        xs[slot, q, 0:own_rows, :] = w_ref[:, q * WIDE:(q + 1) * WIDE]
    pool[z, y, slot] = item_ref[...]
    padding = WIDE - block_rows
    pl.semaphore_wait(barrier, len(peers))

    sent = []

    def send(copy):
        copy.start()
        sent.append(copy)

    for k in (2, 1, 3, 4, 6, 5, 7):
        pair = pl.ds(2 * flip(k)[1], 2)
        send(remote(xs.at[slot, pair], xs.at[slot, pair], xs_s.at[k], xs_r.at[k], line_peer(k)))
    own_e = pool.at[z, y, slot]
    for o in (1, 2, 3):
        send(remote(own_e, own_e, ez_s.at[o - 1], ez_r.at[o - 1], z_peer(o)))

    log_count[...] = jnp.log(counts_ref[...].astype(F32))
    for r in range(positive_ref.shape[0]):
        rows = pl.ds(r * 128, 128)
        line = positive_ref[r:r + 1, :].astype(F32)
        pos_col[rows, :] = jnp.broadcast_to(line, (128, 128)).T
        weight_col[rows, :] = jnp.broadcast_to(weight_ref[r:r + 1, :], (128, 128)).T

    def e_column(o, ox, c):
        xx = (2 * high + low - ox + SIDE) % SIDE
        return pool.at[:, (y - o + SIDE) % SIDE, (xx // 2) * 4 + c * 2 + xx % 2]

    def e_along(o, ox, new_ox, to):
        at = e_column(o, ox, core)
        send(remote(at, at, ex_s.at[new_ox - 1, o], ex_r.at[new_ox - 1, o], x_peer(to)))

    def e_share(o, ox):
        at = e_column(o, ox, core)
        send(remote(at, at, es_s.at[ox, o], es_r.at[ox, o], sibling))

    def e_wait_x(o, ox):
        at = e_column(o, ox, core)
        remote(at, at, ex_s.at[ox - 1, o], ex_r.at[ox - 1, o], sibling).wait_recv()

    for o in (1, 2, 3):
        got = pool.at[(z - o + SIDE) % SIDE, y, slot]
        remote(got, got, ez_s.at[o - 1], ez_r.at[o - 1], z_peer(o)).wait_recv()
    own_column = e_column(0, 0, core)
    for o in (1, 3, 2):
        send(remote(own_column, own_column, ey_s.at[o - 1], ey_r.at[o - 1], y_peer(o)))
    for o in (1, 3):
        e_along(0, 0, o, o)

    def split(k):
        loads[k].wait()
        for n in range(SIDE):
            first = group * (k % 2) + block_rows * n
            hid[SIDE * k + n, :, 0:block_rows] = coeff[:, first:first + block_rows]
            hid[SIDE * k + n, :, block_rows:] = jnp.zeros((coeff.shape[0], padding), BF16)
        if k + 2 < SIDE:
            loads[k + 2].start()
        for n in range(SIDE):
            top = block_rows * n
            hid_t[k, top:top + 128, :] = hid[SIDE * k + n, :, 0:128].T
            hid_t[k, top + 128:top + block_rows, :] = hid[SIDE * k + n, :, 128:256].T[0:block_rows - 128]

    split(0)
    for q in range(QUARTERS):
        wall[q, :, block_rows:WIDE, :] = jnp.zeros((wall.shape[1], padding, WIDE), BF16)

    for k in range(1, LINE):
        got = xs.at[line_slot(k), pl.ds(2 * core, 2)]
        remote(got, got, xs_s.at[k], xs_r.at[k], line_peer(k)).wait_recv()
    half = 4 * own_rows

    def source(row):
        skipped = sum(jnp.where(row >= own_rows * s, 32 - own_rows, 0) for s in (1, 2, 3))
        return row + skipped

    pick = select((half, 128), source)
    here = z * SIDE + y
    for p in range(2):
        q = 2 * core + p
        for h in range(2):
            padded = jnp.reshape(xs[4 * h:4 * h + 4, q], (128, WIDE))
            wall[q, here, half * h:half * (h + 1), :] = dot(pick, padded).astype(BF16)

    def w_block(p, of, og):
        if p == 0:
            b = ((z - og + SIDE) % SIDE) * SIDE + (y - of + SIDE) % SIDE
        else:
            b = ((z - of + SIDE) % SIDE) * SIDE + (y - og + SIDE) % SIDE
        return b

    def w_at(p, of, og, c=None):
        q = 2 * (core if c is None else c) + p
        return wall.at[q, w_block(p, of, og), pl.ds(0, block_rows)]

    def w_send(p, of, og, new_of, new_og, to):
        at = w_at(p, of, og)
        n = new_of * SIDE + new_og
        send(remote(at, at, w_s.at[p, n], w_r.at[p, n], to))

    def w_wait(p, of, og):
        at = w_at(p, of, og)
        n = of * SIDE + og
        remote(at, at, w_s.at[p, n], w_r.at[p, n], sibling).wait_recv()

    def w_share(p, of, og):
        at = w_at(p, of, og)
        n = of * SIDE + og
        send(remote(at, at, ws_s.at[p, n], ws_r.at[p, n], sibling))

    near = ((y_peer, z_peer), (z_peer, y_peer))
    for o in (1, 3, 2):
        for p in range(2):
            w_send(p, 0, 0, o, 0, near[p][0](o))
    for o in (1, 3):
        for p in range(2):
            w_send(p, 0, 0, 0, o, near[p][1](o))
    for p in range(2):
        w_share(p, 0, 0)
    e_share(0, 0)

    split(1)
    for o in (1, 3, 2):
        got = e_column(o, 0, core)
        remote(got, got, ey_s.at[o - 1], ey_r.at[o - 1], y_peer(o)).wait_recv()
        for ox in (1, 3):
            e_along(o, 0, ox, ox)
        e_share(o, 0)
    for of in (1, 3, 2):
        for p in range(2):
            w_wait(p, of, 0)
            for og in (1, 3):
                w_send(p, of, 0, of, og, near[p][1](og))
            w_share(p, of, 0)
    split(2)
    split(3)

    def w_got(p, of, og):
        at = w_at(p, of, og, 1 - core)
        n = of * SIDE + og
        remote(at, at, ws_s.at[p, n], ws_r.at[p, n], sibling).wait_recv()

    half_rows = hid.shape[1] // 2

    def project(p, c, og):
        q = 2 * c + p
        blocks = [w_block(p, of, og) for of in range(SIDE)]

        def rows_of(i, carry):
            rows = pl.ds(pl.multiple_of(i * half_rows, half_rows), half_rows)
            left = jnp.concatenate([hid[b, rows, :] for b in blocks], axis=1)
            right = jnp.concatenate([wall[q, b, 0:WIDE, :] for b in blocks], axis=0)
            value = dot(left, right)
            if og == 0:
                partial[q, rows, :] = value
            elif og == 2:
                queries[rows, columns(q)] = (partial[q, rows, :] + value).astype(BF16)
            else:
                partial[q, rows, :] += value
            return carry

        lax.fori_loop(0, 2, rows_of, 0)

    def columns(q):
        return pl.ds(pl.multiple_of(q * WIDE, WIDE), WIDE)

    def adapt(o):
        yy = (y - o + SIDE) % SIDE
        items = jnp.reshape(pool[:, yy], (SIDE * LINE * item_ref.shape[0], queries.shape[1]))
        value = (items.astype(F32) + dot(items, grad_q[...])).astype(BF16)
        adapted[:, yy] = jnp.reshape(value, (SIDE, LINE * item_ref.shape[0], queries.shape[1]))

    def finish_items(o):
        e_wait_x(o, 2)
        e_share(o, 2)
        for ox in range(SIDE):
            got = e_column(o, ox, 1 - core)
            remote(got, got, es_s.at[ox, o], es_r.at[ox, o], sibling).wait_recv()
        adapt(o)

    loads[SIDE].wait()
    order = (0, 1, 3, 2)
    for n, o in enumerate(order):
        for p in range(2):
            for og in (1, 3):
                w_wait(p, o, og)
                if og == (1 if n < 2 else 3):
                    w_send(p, o, og, o, 2, near[p][1](og))
                w_share(p, o, og)
        for ox in (1, 3):
            e_wait_x(o, ox)
            if ox == (1 if n < 2 else 3):
                e_along(o, ox, 2, 1 if ox == 1 else 3)
            e_share(o, ox)
        if n == 0:
            for p in range(2):
                project(p, core, 0)
        if n == 1:
            for p in range(2):
                for of in range(SIDE):
                    w_got(p, of, 0)
                project(p, 1 - core, 0)
        if n >= 2:
            finish_items(order[n - 2])

    def last(o):
        for p in range(2):
            w_wait(p, o, 2)
            w_share(p, o, 2)

    for p in range(2):
        project(p, core, 1)
    last(0)
    for p in range(2):
        project(p, core, 3)
    last(1)
    finish_items(3)
    last(3)
    for p in range(2):
        for of in range(SIDE):
            w_got(p, of, 1)
        project(p, 1 - core, 1)
    last(2)
    for p in range(2):
        for of in range(SIDE):
            w_got(p, of, 3)
        project(p, 1 - core, 3)
    finish_items(2)

    for p in range(2):
        project(p, core, 2)
    for p in range(2):
        for of in range(SIDE):
            w_got(p, of, 2)
        project(p, 1 - core, 2)

    items_all = log_count.shape[1]

    def all_adapted():
        return jnp.reshape(adapted[...], (items_all, queries.shape[1]))

    def softmax(i, total):
        rows = pl.ds(pl.multiple_of(i * ROWS, ROWS), ROWS)
        logits = scale * dot(queries[rows, :], all_adapted(), (1, 1)) - log_count[...]
        top = jnp.max(logits, axis=1, keepdims=True)
        shifted = jnp.exp(logits - top)
        denom = jnp.sum(shifted, axis=1, keepdims=True)
        lane = lax.broadcasted_iota(jnp.int32, (ROWS, items_all), 1).astype(F32)
        hit = lane == pos_col[rows, 0:1]
        picked = jnp.sum(jnp.where(hit, logits, 0.0), axis=1, keepdims=True)
        weight = weight_col[rows, 0:1]
        losses = jnp.log(denom) + top - picked
        plain = shifted * (weight / denom)
        part = jnp.where(hit, plain - weight, plain).astype(BF16)
        coeff[rows, :] = part
        grad_q[rows, :] = (scale * dot(part, all_adapted())).astype(BF16)
        return total + jnp.sum(weight * losses)

    total = lax.fori_loop(0, queries.shape[0] // ROWS, softmax, jnp.zeros((), F32))

    def loss_send(stage, n, to):
        send(remote(loss_out.at[stage], loss_in.at[stage, n], lo_s.at[stage, n], lo_r.at[stage, n], to))

    def loss_sum(stage, count):
        value = loss_out[stage]
        for n in range(count):
            remote(
                loss_out.at[stage], loss_in.at[stage, n], lo_s.at[stage, n], lo_r.at[stage, n], sibling
            ).wait_recv()
            value = value + loss_in[stage, n]
        return value

    loss_out[0] = jnp.full((8, 128), total, F32)
    loss_send(0, 0, sibling)

    for copy in sent[:-1]:
        copy.wait_send()
    del sent[:-1]

    full = wall.shape[2]
    span = full - block_rows

    def unit(k, q):
        cols = columns(q)
        upper = dot(hid_t[k], grad_q[:, cols])
        lower = dot(pulled[...], queries[:, cols])
        return jnp.reshape(upper, (SIDE, block_rows, WIDE)), jnp.reshape(lower, (SIDE, span, WIDE))

    def sib_copy(p, k, c):
        four = pl.ds(k * SIDE, SIDE)
        return remote(
            wall.at[2 * c + p, four], sib_in.at[p, four], sib_s.at[p, k], sib_r.at[p, k], sibling
        )

    def fz_copy(o):
        four = pl.ds(((z + o) % SIDE) * SIDE, SIDE)
        return remote(wall.at[2 * core, four], first_z.at[o - 1], fz_s.at[o - 1], fz_r.at[o - 1], z_peer(o))

    def fy_copy(k, o):
        b = k * SIDE + (y + o) % SIDE
        n = o - 1
        return remote(wall.at[2 * core + 1, b], first_y.at[n, k], fy_s.at[n, k], fy_r.at[n, k], y_peer(o))

    def reduce_group(i, carry):
        k = (z + 1 + i) % SIDE
        four = pl.ds(k * SIDE, SIDE)
        some = pool[:, :, :, :, pl.ds(pl.multiple_of(k * SIDE * span, SIDE * span), SIDE * span)]
        pulled[...] = dot(coeff[...], jnp.reshape(some, (items_all, SIDE * span))).T.astype(BF16)
        for p in range(2):
            q = 2 * (1 - core) + p
            upper, lower = unit(k, q)
            wall[q, four, 0:block_rows, :] = upper.astype(BF16)
            wall[q, four, block_rows:full, :] = lower.astype(BF16)
            sib_copy(p, k, 1 - core).start()
        for p in range(2):
            q = 2 * core + p
            upper, lower = unit(k, q)
            sib_copy(p, k, 1 - core).wait_recv()
            wall[q, four, 0:block_rows, :] = (upper + sib_in[p, four, 0:block_rows, :].astype(F32)).astype(BF16)
            wall[q, four, block_rows:full, :] = (lower + sib_in[p, four, block_rows:full, :].astype(F32)).astype(BF16)
            if p == 0:
                @pl.when(i < SIDE - 1)
                def _():
                    b = pl.ds(k * SIDE, SIDE)
                    remote(
                        wall.at[2 * core, b], first_z.at[i], fz_s.at[i], fz_r.at[i],
                        device(k, y, high, core, low),
                    ).start()
            else:
                for o in (1, 2, 3):
                    fy_copy(k, o).start()
        return carry

    lax.fori_loop(0, SIDE, reduce_group, 0)

    loss_out[1] = loss_sum(0, 1)
    for o in (1, 2, 3):
        loss_send(1, o - 1, z_peer(o))

    def second_copy(p, o):
        if p == 0:
            b, to = z * SIDE + (y + o) % SIDE, y_peer(o)
        else:
            b, to = ((z + o) % SIDE) * SIDE + y, z_peer(o)
        return remote(
            wall.at[2 * core + p, b], second_in.at[p, o - 1], se_s.at[p, o - 1], se_r.at[p, o - 1], to
        )

    mine = [None, None]
    for o in (1, 2, 3):
        fz_copy(o).wait_recv()
    for o in (1, 2, 3, 0):
        yy = (y + o) % SIDE
        value = wall[2 * core, z * SIDE + yy].astype(F32)
        for n in range(3):
            value = value + first_z[n, yy].astype(F32)
        if o:
            wall[2 * core, z * SIDE + yy] = value.astype(BF16)
            second_copy(0, o).start()
        else:
            mine[0] = value
    for o in (1, 2, 3, 0):
        zz = (z + o) % SIDE
        b = zz * SIDE + y
        value = wall[2 * core + 1, b].astype(F32)
        for n in range(3):
            fy_copy(zz, n + 1).wait_recv()
            value = value + first_y[n, zz].astype(F32)
        if o:
            wall[2 * core + 1, b] = value.astype(BF16)
            second_copy(1, o).start()
        else:
            mine[1] = value

    loss_out[2] = loss_sum(1, 3)
    for o in (1, 2, 3):
        loss_send(2, o - 1, y_peer(o))

    tall = slot_out.shape[2]
    shape = (LINE * tall, full)
    row = lax.broadcasted_iota(jnp.int32, shape, 0)
    col = lax.broadcasted_iota(jnp.int32, shape, 1)
    owner = sum(jnp.where(row >= tall * s, 1, 0) for s in range(1, LINE))
    inner = row - tall * owner
    from_w = (inner < own_rows) & (col == own_rows * owner + inner)
    from_a = (inner >= 32) & (inner < 32 + adapter_rows) & (col == block_rows + adapter_rows * owner + inner - 32)
    spread = jnp.where(from_w | from_a, 1.0, 0.0).astype(BF16)
    for p in range(2):
        value = mine[p]
        for o in (1, 2, 3):
            second_copy(p, o).wait_recv()
            value = value + second_in[p, o - 1].astype(F32)
        slots = dot(spread, value.astype(BF16)).astype(BF16)
        slot_out[p] = jnp.reshape(slots, (LINE, tall, WIDE))

    def slot_copy(k):
        return remote(
            slot_out.at[:, line_slot(k)], slot_in.at[k], sl_s.at[k], sl_r.at[k], line_peer(k)
        )

    for k in (1, 4, 5, 3, 6, 7, 2):
        slot_copy(k).start()

    loss_out[3] = loss_sum(2, 3)
    for n, k in enumerate((1, 4, 5)):
        loss_send(3, n, line_peer(k))

    for k in range(1, LINE):
        slot_copy(k).wait_recv()
    for p in range(2):
        same = slot_out[p, slot].astype(F32)
        for k in (1, 4, 5):
            same = same + slot_in[k, p].astype(F32)
        other = slot_in[2, p].astype(F32)
        for k in (3, 6, 7):
            other = other + slot_in[k, p].astype(F32)
        for value, c in ((same, core), (other, 1 - core)):
            cols = pl.ds(pl.multiple_of((2 * c + p) * WIDE, WIDE), WIDE)
            gw_ref[:, cols] = value[0:own_rows]
            ga_ref[:, cols] = scale * value[32:32 + adapter_rows]

    loss_ref[...] = loss_sum(3, 3)

    for copy in sent:
        copy.wait_send()
    for p in range(2):
        for k in range(SIDE):
            sib_copy(p, k, 1 - core).wait_send()
    for o in (1, 2, 3):
        fz_copy(o).wait_send()
        for k in range(SIDE):
            fy_copy(k, o).wait_send()
        for p in range(2):
            second_copy(p, o).wait_send()
    for k in range(1, LINE):
        slot_copy(k).wait_send()


def finish_kernel(share, gw_in, ga_in, loss_in, gw_ref, ga_ref, loss_ref):
    gw_ref[...] = gw_in[...]
    ga_ref[...] = ga_in[...]
    loss_ref[...] = loss_in[0:1, 0:1] * share


def on_device(hidden, w_query, adapter, item_emb, counts, positive, loss_weight):
    scale = 2.0 / math.sqrt(adapter.shape[0])
    devices = lax.axis_size(AXES)
    queries, deep = hidden.shape
    wide = adapter.shape[0]
    items = counts.shape[0]
    block = LINE * w_query.shape[0]
    full = block + LINE * (wide // devices)
    sem = pltpu.SemaphoreType.DMA
    vmem = pl.BlockSpec(memory_space=pltpu.VMEM)
    anywhere = pl.BlockSpec(memory_space=pl.ANY)
    gw, ga, loss = pl.pallas_call(
        functools.partial(step_kernel, scale),
        out_shape=(
            jax.ShapeDtypeStruct((w_query.shape[0], wide), F32),
            jax.ShapeDtypeStruct((wide // devices, wide), F32),
            jax.ShapeDtypeStruct((8, 128), F32),
        ),
        in_specs=[anywhere, vmem, anywhere, vmem, vmem, vmem, vmem],
        out_specs=(vmem, vmem, vmem),
        scratch_shapes=[
            pltpu.VMEM((16, queries, WIDE), BF16),
            pltpu.VMEM((SIDE, deep // SIDE, queries), BF16),
            pltpu.VMEM((QUARTERS, 16, full, WIDE), BF16),
            pltpu.VMEM((LINE, QUARTERS, 32, WIDE), BF16),
            pltpu.VMEM((SIDE, SIDE, LINE, items // devices, wide), BF16),
            pltpu.VMEM((SIDE, SIDE, LINE * (items // devices), wide), BF16),
            pltpu.VMEM((QUARTERS, queries, WIDE), F32),
            pltpu.VMEM((queries, wide), BF16),
            pltpu.VMEM((queries, items), BF16),
            pltpu.VMEM((queries, wide), BF16),
            pltpu.VMEM((wide // SIDE, queries), BF16),
            pltpu.VMEM((queries, 128), F32),
            pltpu.VMEM((queries, 128), F32),
            pltpu.VMEM((1, items), F32),
            pltpu.VMEM((2, 16, full, WIDE), BF16),
            pltpu.VMEM((3, SIDE, full, WIDE), BF16),
            pltpu.VMEM((3, SIDE, full, WIDE), BF16),
            pltpu.VMEM((2, 3, full, WIDE), BF16),
            pltpu.VMEM((2, LINE, 48, WIDE), BF16),
            pltpu.VMEM((LINE, 2, 48, WIDE), BF16),
            pltpu.VMEM((4, 8, 128), F32),
            pltpu.VMEM((4, 3, 8, 128), F32),
            sem((SIDE + 1,)),
            sem((LINE,)), sem((LINE,)),
            sem((2, 16)), sem((2, 16)),
            sem((2, 16)), sem((2, 16)),
            sem((3,)), sem((3,)),
            sem((3,)), sem((3,)),
            sem((3, SIDE)), sem((3, SIDE)),
            sem((SIDE, SIDE)), sem((SIDE, SIDE)),
            sem((2, SIDE)), sem((2, SIDE)),
            sem((3,)), sem((3,)),
            sem((3, SIDE)), sem((3, SIDE)),
            sem((2, 3)), sem((2, 3)),
            sem((LINE,)), sem((LINE,)),
            sem((4, 3)), sem((4, 3)),
        ],
        compiler_params=pltpu.CompilerParams(
            collective_id=0, has_side_effects=True, vmem_limit_bytes=64 * 1024 * 1024 - 65536
        ),
        name="sampled_softmax_step",
    )(
        hidden, w_query, adapter, item_emb, counts.reshape(1, items),
        positive.reshape(queries // 128, 128), loss_weight.reshape(queries // 128, 128),
    )
    gw, ga, loss = pl.pallas_call(
        functools.partial(finish_kernel, 1.0 / (queries * devices)),
        out_shape=(
            jax.ShapeDtypeStruct(gw.shape, F32),
            jax.ShapeDtypeStruct(ga.shape, F32),
            jax.ShapeDtypeStruct((1, 1), F32),
        ),
        in_specs=[vmem, vmem, vmem],
        out_specs=(vmem, vmem, vmem),
        name="finish",
    )(gw, ga, loss)
    return gw, ga, loss.reshape(())


def solution(mesh):
    placed = (P(AXES, None), P(AXES, None), P(), P(AXES, None), P(), P(AXES), P(AXES))
    return jax.shard_map(
        on_device,
        mesh=mesh,
        in_specs=placed,
        out_specs=(P(AXES, None), P(AXES, None), P()),
        check_vma=False,
    )
```

```python
import functools
import math

import jax
import jax.numpy as jnp
from jax import lax
from jax.experimental import pallas as pl
from jax.experimental.pallas import tpu as pltpu
from jax.sharding import PartitionSpec as P

MESH = pl.DeviceIdType.MESH
F32, BF16 = jnp.float32, jnp.bfloat16
AXES = ("item", "qgrp")
LINE = 8
SIDE = 4
QUARTERS, WIDE = 4, 256
ROWS = 256


def dot(a, b, contract=(1, 0)):
    dims = (((contract[0],), (contract[1],)), ((), ()))
    return lax.dot_general(a, b, dims, preferred_element_type=F32)


def place():
    item, low = lax.axis_index("item"), lax.axis_index("qgrp")
    return item // 16, (item // 4) % 4, (item // 2) % 2, item % 2, low


def device(z, y, high, core, low):
    return (z * 16 + y * 4 + high * 2 + core, low)


def select(shape, source):
    row = lax.broadcasted_iota(jnp.int32, shape, 0)
    col = lax.broadcasted_iota(jnp.int32, shape, 1)
    return jnp.where(col == source(row), 1.0, 0.0).astype(BF16)


def step_kernel(
    scale, hidden_ref, w_ref, adapter_ref, item_ref, counts_ref, positive_ref, weight_ref,
    gw_ref, ga_ref, loss_ref,
    hid, hid_t, wall, xs, pool, adapted, partial, queries, coeff, grad_q, pulled, pos_col, weight_col, log_count,
    sib_in, ga_sib, rz_in, lz_in, ry_in, ly_in, gx_in, gy_out, gy_in, gz_out, gz_in, g_out, g_in, shuffle,
    second_in, slot_out, slot_in, loss_out, loss_in,
    load_sem, xs_s, xs_r, w_s, w_r, ws_s, ws_r, ez_s, ez_r, ey_s, ey_r, ex_s, ex_r, es_s, es_r, sib_s, sib_r, gs_s, gs_r, rz_s, rz_r, lz_s, lz_r, ry_s, ry_r,
    ly_s, ly_r, gx_s, gx_r, gy_s, gy_r, gz_s, gz_r, g_s, g_r, se_s, se_r,
    sl_s, sl_r, lo_s, lo_r,
):
    z, y, high, core, low = place()
    slot = high * 4 + core * 2 + low
    block_rows = LINE * w_ref.shape[0]
    own_rows = w_ref.shape[0]
    adapter_rows = ga_ref.shape[0]
    group = SIDE * block_rows
    sibling = device(z, y, high, 1 - core, low)

    def z_peer(o):
        return device((z + o) % SIDE, y, high, core, low)

    def x_peer(o):
        xx = (2 * high + low + o) % SIDE
        return device(z, y, xx // 2, core, xx % 2)

    def y_peer(o):
        return device(z, (y + o) % SIDE, high, core, low)

    def flip(k):
        return (high + k // 4) % 2, (core + (k // 2) % 2) % 2, (low + k % 2) % 2

    def line_peer(k):
        h, c, l = flip(k)
        return device(z, y, h, c, l)

    def line_slot(k):
        h, c, l = flip(k)
        return h * 4 + c * 2 + l

    def remote(src, dst, send, recv, to):
        return pltpu.make_async_remote_copy(
            src_ref=src, dst_ref=dst, send_sem=send, recv_sem=recv, device_id=to, device_id_type=MESH
        )

    loads = [
        pltpu.make_async_copy(
            hidden_ref.at[:, pl.ds(group * k, group)], coeff.at[:, pl.ds(group * (k % 2), group)], load_sem.at[k]
        )
        for k in range(SIDE)
    ]
    loads.append(pltpu.make_async_copy(adapter_ref, grad_q, load_sem.at[SIDE]))
    for k in (0, 1, SIDE):
        loads[k].start()

    barrier = pltpu.get_barrier_semaphore()
    peers = [line_peer(k) for k in range(1, LINE)]
    peers += [z_peer(o) for o in (1, 2, 3)] + [y_peer(o) for o in (1, 2, 3)]
    for peer in peers:
        pl.semaphore_signal(barrier, inc=1, device_id=peer, device_id_type=MESH)

    xs[slot, :, own_rows:, :] = jnp.zeros((QUARTERS, 32 - own_rows, WIDE), BF16)
    for q in range(QUARTERS):
        xs[slot, q, 0:own_rows, :] = w_ref[:, q * WIDE:(q + 1) * WIDE]
    pool[z, y, slot] = item_ref[...]
    padding = WIDE - block_rows
    pl.semaphore_wait(barrier, len(peers))

    sent = []

    def send(copy):
        copy.start()
        sent.append(copy)

    for k in (2, 1, 3, 4, 6, 5, 7):
        pair = pl.ds(2 * flip(k)[1], 2)
        send(remote(xs.at[slot, pair], xs.at[slot, pair], xs_s.at[k], xs_r.at[k], line_peer(k)))
    own_e = pool.at[z, y, slot]
    for o in (1, 2, 3):
        send(remote(own_e, own_e, ez_s.at[o - 1], ez_r.at[o - 1], z_peer(o)))

    log_count[...] = jnp.log(counts_ref[...].astype(F32))
    for r in range(positive_ref.shape[0]):
        rows = pl.ds(r * 128, 128)
        line = positive_ref[r:r + 1, :].astype(F32)
        pos_col[rows, :] = jnp.broadcast_to(line, (128, 128)).T
        weight_col[rows, :] = jnp.broadcast_to(weight_ref[r:r + 1, :], (128, 128)).T

    def e_column(o, ox, c):
        xx = (2 * high + low - ox + SIDE) % SIDE
        return pool.at[:, (y - o + SIDE) % SIDE, (xx // 2) * 4 + c * 2 + xx % 2]

    def e_along(o, ox, new_ox, to):
        at = e_column(o, ox, core)
        send(remote(at, at, ex_s.at[new_ox - 1, o], ex_r.at[new_ox - 1, o], x_peer(to)))

    def e_share(o, ox):
        at = e_column(o, ox, core)
        send(remote(at, at, es_s.at[ox, o], es_r.at[ox, o], sibling))

    def e_wait_x(o, ox):
        at = e_column(o, ox, core)
        remote(at, at, ex_s.at[ox - 1, o], ex_r.at[ox - 1, o], sibling).wait_recv()

    for o in (1, 2, 3):
        got = pool.at[(z - o + SIDE) % SIDE, y, slot]
        remote(got, got, ez_s.at[o - 1], ez_r.at[o - 1], z_peer(o)).wait_recv()
    own_column = e_column(0, 0, core)
    for o in (1, 3, 2):
        send(remote(own_column, own_column, ey_s.at[o - 1], ey_r.at[o - 1], y_peer(o)))
    for o in (1, 3):
        e_along(0, 0, o, o)

    def split(k):
        loads[k].wait()
        for n in range(SIDE):
            first = group * (k % 2) + block_rows * n
            hid[SIDE * k + n, :, 0:block_rows] = coeff[:, first:first + block_rows]
            hid[SIDE * k + n, :, block_rows:] = jnp.zeros((coeff.shape[0], padding), BF16)
        if k + 2 < SIDE:
            loads[k + 2].start()
        for n in range(SIDE):
            top = block_rows * n
            hid_t[k, top:top + 128, :] = hid[SIDE * k + n, :, 0:128].T
            hid_t[k, top + 128:top + block_rows, :] = hid[SIDE * k + n, :, 128:256].T[0:block_rows - 128]

    split(0)
    for q in range(QUARTERS):
        wall[q, :, block_rows:WIDE, :] = jnp.zeros((wall.shape[1], padding, WIDE), BF16)

    for k in range(1, LINE):
        got = xs.at[line_slot(k), pl.ds(2 * core, 2)]
        remote(got, got, xs_s.at[k], xs_r.at[k], line_peer(k)).wait_recv()
    half = 4 * own_rows

    def source(row):
        skipped = sum(jnp.where(row >= own_rows * s, 32 - own_rows, 0) for s in (1, 2, 3))
        return row + skipped

    pick = select((half, 128), source)
    here = z * SIDE + y
    for p in range(2):
        q = 2 * core + p
        for h in range(2):
            padded = jnp.reshape(xs[4 * h:4 * h + 4, q], (128, WIDE))
            wall[q, here, half * h:half * (h + 1), :] = dot(pick, padded).astype(BF16)

    def w_block(p, of, og):
        if p == 0:
            b = ((z - og + SIDE) % SIDE) * SIDE + (y - of + SIDE) % SIDE
        else:
            b = ((z - of + SIDE) % SIDE) * SIDE + (y - og + SIDE) % SIDE
        return b

    def w_at(p, of, og, c=None):
        q = 2 * (core if c is None else c) + p
        return wall.at[q, w_block(p, of, og), pl.ds(0, block_rows)]

    def w_send(p, of, og, new_of, new_og, to):
        at = w_at(p, of, og)
        n = new_of * SIDE + new_og
        send(remote(at, at, w_s.at[p, n], w_r.at[p, n], to))

    def w_wait(p, of, og):
        at = w_at(p, of, og)
        n = of * SIDE + og
        remote(at, at, w_s.at[p, n], w_r.at[p, n], sibling).wait_recv()

    def w_share(p, of, og):
        at = w_at(p, of, og)
        n = of * SIDE + og
        send(remote(at, at, ws_s.at[p, n], ws_r.at[p, n], sibling))

    near = ((y_peer, z_peer), (z_peer, y_peer))
    for o in (1, 3, 2):
        for p in range(2):
            w_send(p, 0, 0, o, 0, near[p][0](o))
    for o in (1, 3):
        for p in range(2):
            w_send(p, 0, 0, 0, o, near[p][1](o))
    for p in range(2):
        w_share(p, 0, 0)
    e_share(0, 0)

    split(1)
    for o in (1, 3, 2):
        got = e_column(o, 0, core)
        remote(got, got, ey_s.at[o - 1], ey_r.at[o - 1], y_peer(o)).wait_recv()
        for ox in (1, 3):
            e_along(o, 0, ox, ox)
        e_share(o, 0)
    for of in (1, 3, 2):
        for p in range(2):
            w_wait(p, of, 0)
            for og in (1, 3):
                w_send(p, of, 0, of, og, near[p][1](og))
            w_share(p, of, 0)
    split(2)
    split(3)

    def w_got(p, of, og):
        at = w_at(p, of, og, 1 - core)
        n = of * SIDE + og
        remote(at, at, ws_s.at[p, n], ws_r.at[p, n], sibling).wait_recv()

    half_rows = hid.shape[1] // 2

    def project(p, c, og):
        q = 2 * c + p
        blocks = [w_block(p, of, og) for of in range(SIDE)]

        def rows_of(i, carry):
            rows = pl.ds(pl.multiple_of(i * half_rows, half_rows), half_rows)
            left = jnp.concatenate([hid[b, rows, :] for b in blocks], axis=1)
            right = jnp.concatenate([wall[q, b, 0:WIDE, :] for b in blocks], axis=0)
            value = dot(left, right)
            if og == 0:
                partial[q, rows, :] = value
            elif og == 2:
                queries[rows, columns(q)] = (partial[q, rows, :] + value).astype(BF16)
            else:
                partial[q, rows, :] += value
            return carry

        lax.fori_loop(0, 2, rows_of, 0)

    def columns(q):
        return pl.ds(pl.multiple_of(q * WIDE, WIDE), WIDE)

    def adapt(o):
        yy = (y - o + SIDE) % SIDE
        items = jnp.reshape(pool[:, yy], (SIDE * LINE * item_ref.shape[0], queries.shape[1]))
        value = (items.astype(F32) + dot(items, grad_q[...])).astype(BF16)
        adapted[:, yy] = jnp.reshape(value, (SIDE, LINE * item_ref.shape[0], queries.shape[1]))

    def finish_items(o):
        e_wait_x(o, 2)
        e_share(o, 2)
        for ox in range(SIDE):
            got = e_column(o, ox, 1 - core)
            remote(got, got, es_s.at[ox, o], es_r.at[ox, o], sibling).wait_recv()
        adapt(o)

    loads[SIDE].wait()
    order = (0, 1, 3, 2)
    for n, o in enumerate(order):
        for p in range(2):
            for og in (1, 3):
                w_wait(p, o, og)
                if og == (1 if n < 2 else 3):
                    w_send(p, o, og, o, 2, near[p][1](og))
                w_share(p, o, og)
        for ox in (1, 3):
            e_wait_x(o, ox)
            if ox == (1 if n < 2 else 3):
                e_along(o, ox, 2, 1 if ox == 1 else 3)
            e_share(o, ox)
        if n == 0:
            for p in range(2):
                project(p, core, 0)
        if n == 1:
            for p in range(2):
                for of in range(SIDE):
                    w_got(p, of, 0)
                project(p, 1 - core, 0)
        if n >= 2:
            finish_items(order[n - 2])

    def last(o):
        for p in range(2):
            w_wait(p, o, 2)
            w_share(p, o, 2)

    for p in range(2):
        project(p, core, 1)
    last(0)
    for p in range(2):
        project(p, core, 3)
    last(1)
    finish_items(3)
    last(3)
    for p in range(2):
        for of in range(SIDE):
            w_got(p, of, 1)
        project(p, 1 - core, 1)
    last(2)
    for p in range(2):
        for of in range(SIDE):
            w_got(p, of, 3)
        project(p, 1 - core, 3)
    finish_items(2)

    for p in range(2):
        project(p, core, 2)
    for p in range(2):
        for of in range(SIDE):
            w_got(p, of, 2)
        project(p, 1 - core, 2)

    items_all = log_count.shape[1]

    def all_adapted():
        return jnp.reshape(adapted[...], (items_all, queries.shape[1]))

    def softmax(i, total):
        rows = pl.ds(pl.multiple_of(i * ROWS, ROWS), ROWS)
        logits = scale * dot(queries[rows, :], all_adapted(), (1, 1)) - log_count[...]
        top = jnp.max(logits, axis=1, keepdims=True)
        shifted = jnp.exp(logits - top)
        denom = jnp.sum(shifted, axis=1, keepdims=True)
        lane = lax.broadcasted_iota(jnp.int32, (ROWS, items_all), 1).astype(F32)
        hit = lane == pos_col[rows, 0:1]
        picked = jnp.sum(jnp.where(hit, logits, 0.0), axis=1, keepdims=True)
        weight = weight_col[rows, 0:1]
        losses = jnp.log(denom) + top - picked
        plain = shifted * (weight / denom)
        part = jnp.where(hit, plain - weight, plain).astype(BF16)
        coeff[rows, :] = part
        grad_q[rows, :] = (scale * dot(part, all_adapted())).astype(BF16)
        return total + jnp.sum(weight * losses)

    total = lax.fori_loop(0, queries.shape[0] // ROWS, softmax, jnp.zeros((), F32))

    def loss_send(stage, n, to):
        send(remote(loss_out.at[stage], loss_in.at[stage, n], lo_s.at[stage, n], lo_r.at[stage, n], to))

    def loss_sum(stage, count):
        value = loss_out[stage]
        for n in range(count):
            remote(
                loss_out.at[stage], loss_in.at[stage, n], lo_s.at[stage, n], lo_r.at[stage, n], sibling
            ).wait_recv()
            value = value + loss_in[stage, n]
        return value

    loss_out[0] = jnp.full((8, 128), total, F32)
    loss_send(0, 0, sibling)

    for copy in sent[:-1]:
        copy.wait_send()
    del sent[:-1]

    span = SIDE * LINE * adapter_rows
    valid = pl.ds(0, block_rows)
    first, second = 2 * core, 2 * core + 1

    def sib_copy(p, k):
        four = pl.ds(k * SIDE, SIDE)
        src = wall.at[2 * (1 - core) + p, four, valid]
        return remote(src, sib_in.at[p, four], sib_s.at[p, k], sib_r.at[p, k], sibling)

    def ga_sib_copy(p, k):
        src = hid.at[SIDE * (2 * (1 - core) + p) + k, pl.ds(0, span)]
        return remote(src, ga_sib.at[p, k], gs_s.at[p, k], gs_r.at[p, k], sibling)

    def ring_z(o):
        k = (z + 2) % SIDE
        n = 0 if o == 1 else 1
        src = wall.at[first, pl.ds(SIDE * k + 2 * n, 2), valid]
        return remote(src, rz_in.at[n], rz_s.at[n], rz_r.at[n], z_peer(o))

    def last_z(o, h):
        k = (z + o) % SIDE
        n = 0 if o == 1 else 1
        src = wall.at[first, pl.ds(SIDE * k + 2 * h, 2), valid]
        return remote(src, lz_in.at[n, pl.ds(2 * h, 2)], lz_s.at[n, h], lz_r.at[n, h], z_peer(o))

    def ring_y(i, k):
        b = SIDE * k + (y + 2) % SIDE
        to = y_peer(1 if i < 2 else 3)
        return remote(wall.at[second, b, valid], ry_in.at[i], ry_s.at[i], ry_r.at[i], to)

    def last_y(i, k, o):
        b = SIDE * k + (y + o) % SIDE
        n = 0 if o == 1 else 1
        return remote(wall.at[second, b, valid], ly_in.at[n, i], ly_s.at[n, i], ly_r.at[n, i], y_peer(o))

    def gx_copy(k, p, o):
        xx = (2 * high + low + o) % SIDE
        rows = pl.ds(pl.multiple_of(xx * (span // SIDE), span // SIDE), span // SIDE)
        src = hid.at[SIDE * (first + p) + k, rows]
        return remote(src, gx_in.at[o - 1, p, k], gx_s.at[o - 1, p, k], gx_r.at[o - 1, p, k], x_peer(o))

    row = lax.broadcasted_iota(jnp.int32, (span, span), 0)
    col = lax.broadcasted_iota(jnp.int32, (span, span), 1)
    from_row = ((row >> 4) & 3) * 64 + (row >> 7) * 32 + ((row >> 3) & 1) * 16 + ((row >> 6) & 1) * 8 + (row & 7)
    shuffle[...] = jnp.where(col == from_row, 1.0, 0.0).astype(BF16)

    hops = (2, 1, 3, 0)
    for i, hop in enumerate(hops):
        k = (z + hop) % SIDE
        four = pl.ds(k * SIDE, SIDE)

        def weight_rows(q, k=k):
            return jnp.reshape(dot(hid_t[k], grad_q[:, columns(q)]), (SIDE, block_rows, WIDE))

        def for_sibling(p, carry, k=k, four=four):
            q = 2 * (1 - core) + p
            wall[q, four, 0:block_rows, :] = weight_rows(q).astype(BF16)
            sib_copy(p, k).start()
            return carry

        def for_self(p, carry, k=k, four=four):
            q = 2 * core + p
            value = weight_rows(q)
            sib_copy(p, k).wait_recv()
            wall[q, four, 0:block_rows, :] = (value + sib_in[p, four].astype(F32)).astype(BF16)
            return carry

        lax.fori_loop(0, 2, for_sibling, 0)
        lax.fori_loop(0, 2, for_self, 0)

        if hop == 2:
            ring_z(1).start()
            ring_z(3).start()
        elif hop:
            last_z(hop, 1 if hop == 1 else 0).start()
        ring_y(i, k).start()
        last_y(i, k, 3 if i < 2 else 1).start()

        some = pool[:, :, :, :, pl.ds(pl.multiple_of(k * span, span), span)]
        pulled[...] = dot(coeff[...], jnp.reshape(some, (items_all, span))).T.astype(BF16)

        if hop in (1, 3):
            h = 0 if hop == 1 else 1
            ring_z(hop).wait_recv()
            for n in range(2):
                b = SIDE * k + 2 * h + n
                total_rows = wall[first, b, 0:block_rows, :].astype(F32) + rz_in[h, n].astype(F32)
                wall[first, b, 0:block_rows, :] = total_rows.astype(BF16)
            last_z(hop, h).start()

        def adapter_sibling(p, carry, k=k):
            q = 2 * (1 - core) + p
            hid[SIDE * q + k, 0:span, :] = dot(pulled[...], queries[:, columns(q)]).astype(BF16)
            ga_sib_copy(p, k).start()
            return carry

        def adapter_self(p, carry, k=k):
            q = 2 * core + p
            value = dot(pulled[...], queries[:, columns(q)])
            ga_sib_copy(p, k).wait_recv()
            value = (value + ga_sib[p, k].astype(F32)).astype(BF16)
            hid[SIDE * q + k, 0:span, :] = dot(shuffle[...], value).astype(BF16)
            for o in (1, 3, 2):
                gx_copy(k, p, o).start()
            return carry

        lax.fori_loop(0, 2, adapter_sibling, 0)
        lax.fori_loop(0, 2, adapter_self, 0)

        o = 1 if i < 2 else 3
        ring_y(i, k).wait_recv()
        b = SIDE * k + (y + o) % SIDE
        total_rows = wall[second, b, 0:block_rows, :].astype(F32) + ry_in[i].astype(F32)
        wall[second, b, 0:block_rows, :] = total_rows.astype(BF16)
        last_y(i, k, o).start()

    loss_out[1] = loss_sum(0, 1)
    for o in (1, 2, 3):
        loss_send(1, o - 1, z_peer(o))

    def second_copy(p, o):
        if p == 0:
            b, to = z * SIDE + (y + o) % SIDE, y_peer(o)
        else:
            b, to = ((z + o) % SIDE) * SIDE + y, z_peer(o)
        src = wall.at[2 * core + p, b, valid]
        return remote(src, second_in.at[p, o - 1], se_s.at[p, o - 1], se_r.at[p, o - 1], to)

    mine = [None, None]
    for o in (1, 3):
        for h in range(2):
            last_z(o, h).wait_recv()
    for o in (1, 2, 3, 0):
        yy = (y + o) % SIDE
        b = z * SIDE + yy
        value = wall[first, b, 0:block_rows, :].astype(F32) + lz_in[0, yy].astype(F32) + lz_in[1, yy].astype(F32)
        if o:
            wall[first, b, 0:block_rows, :] = value.astype(BF16)
            second_copy(0, o).start()
        else:
            mine[0] = value
    for i, hop in enumerate(hops):
        k = (z + hop) % SIDE
        b = k * SIDE + y
        last_y(i, k, 1).wait_recv()
        last_y(i, k, 3).wait_recv()
        value = wall[second, b, 0:block_rows, :].astype(F32) + ly_in[0, i].astype(F32) + ly_in[1, i].astype(F32)
        if hop:
            wall[second, b, 0:block_rows, :] = value.astype(BF16)
            second_copy(1, hop).start()
        else:
            mine[1] = value

    loss_out[2] = loss_sum(1, 3)
    for o in (1, 2, 3):
        loss_send(2, o - 1, y_peer(o))

    def gy_copy(o):
        return remote(gy_out.at[(y + o) % SIDE], gy_in.at[o - 1], gy_s.at[o - 1], gy_r.at[o - 1], y_peer(o))

    def gz_copy(o):
        return remote(gz_out.at[(z + o) % SIDE], gz_in.at[o - 1], gz_s.at[o - 1], gz_r.at[o - 1], z_peer(o))

    pair = 2 * adapter_rows
    quarter_rows = span // SIDE
    here_x = pl.ds(pl.multiple_of((2 * high + low) * quarter_rows, quarter_rows), quarter_rows)
    for k in range(SIDE):
        for p in range(2):
            value = hid[SIDE * (first + p) + k, here_x, :].astype(F32)
            for o in (1, 2, 3):
                gx_copy(k, p, o).wait_recv()
                value = value + gx_in[o - 1, p, k].astype(F32)
            value = value.astype(BF16)
            for yy in range(SIDE):
                gy_out[yy, p, k] = value[pair * yy:pair * (yy + 1)]
    for o in (1, 2, 3):
        gy_copy(o).start()

    tall = slot_out.shape[2]
    shape = (LINE * tall, block_rows)
    row = lax.broadcasted_iota(jnp.int32, shape, 0)
    col = lax.broadcasted_iota(jnp.int32, shape, 1)
    owner, inner = row >> 5, row & 31
    spread = jnp.where((inner < own_rows) & (col == own_rows * owner + inner), 1.0, 0.0).astype(BF16)
    for p in range(2):
        value = mine[p]
        for o in (1, 2, 3):
            second_copy(p, o).wait_recv()
            value = value + second_in[p, o - 1].astype(F32)
        slots = dot(spread, value.astype(BF16)).astype(BF16)
        slot_out[p] = jnp.reshape(slots, (LINE, tall, WIDE))

    def slot_copy(k):
        return remote(
            slot_out.at[:, line_slot(k)], slot_in.at[k], sl_s.at[k], sl_r.at[k], line_peer(k)
        )

    for k in (4, 1, 5, 6, 3, 7, 2):
        slot_copy(k).start()

    for o in (1, 2, 3):
        gy_copy(o).wait_recv()
    value = gy_out[y].astype(F32)
    for o in (1, 2, 3):
        value = value + gy_in[o - 1].astype(F32)
    value = value.astype(BF16)
    for k in range(SIDE):
        gz_out[k] = value[:, k]
    for o in (1, 2, 3):
        gz_copy(o).start()

    loss_out[3] = loss_sum(2, 3)
    for n, k in enumerate((1, 4, 5)):
        loss_send(3, n, line_peer(k))

    for o in (1, 2, 3):
        gz_copy(o).wait_recv()
    value = gz_out[z].astype(F32)
    for o in (1, 2, 3):
        value = value + gz_in[o - 1].astype(F32)
    for c in range(2):
        g_out[c] = value[:, c * adapter_rows:(c + 1) * adapter_rows]
    g_copy = remote(g_out.at[1 - core], g_in, g_s, g_r, sibling)
    g_copy.start()

    for k in range(1, LINE):
        slot_copy(k).wait_recv()
    for p in range(2):
        same = slot_out[p, slot].astype(F32)
        for k in (1, 4, 5):
            same = same + slot_in[k, p].astype(F32)
        other = slot_in[2, p].astype(F32)
        for k in (3, 6, 7):
            other = other + slot_in[k, p].astype(F32)
        gw_ref[:, columns(2 * core + p)] = same[0:own_rows]
        gw_ref[:, columns(2 * (1 - core) + p)] = other[0:own_rows]

    g_copy.wait_recv()
    for p in range(2):
        ga_ref[:, columns(2 * core + p)] = scale * g_out[core, p]
        ga_ref[:, columns(2 * (1 - core) + p)] = scale * g_in[p]

    loss_ref[...] = loss_sum(3, 3)

    for copy in sent:
        copy.wait_send()
    g_copy.wait_send()
    for i, hop in enumerate(hops):
        k = (z + hop) % SIDE
        ring_y(i, k).wait_send()
        for o in (1, 3):
            last_y(i, k, o).wait_send()
        for p in range(2):
            sib_copy(p, k).wait_send()
            ga_sib_copy(p, k).wait_send()
            for o in (1, 2, 3):
                gx_copy(k, p, o).wait_send()
    for o in (1, 3):
        ring_z(o).wait_send()
        for h in range(2):
            last_z(o, h).wait_send()
    for o in (1, 2, 3):
        gy_copy(o).wait_send()
        gz_copy(o).wait_send()
        for p in range(2):
            second_copy(p, o).wait_send()
    for k in range(1, LINE):
        slot_copy(k).wait_send()


def finish_kernel(share, gw_in, ga_in, loss_in, gw_ref, ga_ref, loss_ref):
    gw_ref[...] = gw_in[...]
    ga_ref[...] = ga_in[...]
    loss_ref[...] = loss_in[0:1, 0:1] * share


def on_device(hidden, w_query, adapter, item_emb, counts, positive, loss_weight):
    scale = 2.0 / math.sqrt(adapter.shape[0])
    devices = lax.axis_size(AXES)
    queries, deep = hidden.shape
    wide = adapter.shape[0]
    items = counts.shape[0]
    block = LINE * w_query.shape[0]
    span = wide // SIDE
    sem = pltpu.SemaphoreType.DMA
    vmem = pl.BlockSpec(memory_space=pltpu.VMEM)
    anywhere = pl.BlockSpec(memory_space=pl.ANY)
    gw, ga, loss = pl.pallas_call(
        functools.partial(step_kernel, scale),
        out_shape=(
            jax.ShapeDtypeStruct((w_query.shape[0], wide), F32),
            jax.ShapeDtypeStruct((wide // devices, wide), F32),
            jax.ShapeDtypeStruct((8, 128), F32),
        ),
        in_specs=[anywhere, vmem, anywhere, vmem, vmem, vmem, vmem],
        out_specs=(vmem, vmem, vmem),
        scratch_shapes=[
            pltpu.VMEM((16, queries, WIDE), BF16),
            pltpu.VMEM((SIDE, deep // SIDE, queries), BF16),
            pltpu.VMEM((QUARTERS, 16, WIDE, WIDE), BF16),
            pltpu.VMEM((LINE, QUARTERS, 32, WIDE), BF16),
            pltpu.VMEM((SIDE, SIDE, LINE, items // devices, wide), BF16),
            pltpu.VMEM((SIDE, SIDE, LINE * (items // devices), wide), BF16),
            pltpu.VMEM((QUARTERS, queries, WIDE), F32),
            pltpu.VMEM((queries, wide), BF16),
            pltpu.VMEM((queries, items), BF16),
            pltpu.VMEM((queries, wide), BF16),
            pltpu.VMEM((wide // SIDE, queries), BF16),
            pltpu.VMEM((queries, 128), F32),
            pltpu.VMEM((queries, 128), F32),
            pltpu.VMEM((1, items), F32),
            pltpu.VMEM((2, 16, block, WIDE), BF16),
            pltpu.VMEM((2, SIDE, span, WIDE), BF16),
            pltpu.VMEM((2, 2, block, WIDE), BF16),
            pltpu.VMEM((2, SIDE, block, WIDE), BF16),
            pltpu.VMEM((SIDE, block, WIDE), BF16),
            pltpu.VMEM((2, SIDE, block, WIDE), BF16),
            pltpu.VMEM((3, 2, SIDE, span // SIDE, WIDE), BF16),
            pltpu.VMEM((SIDE, 2, SIDE, span // 16, WIDE), BF16),
            pltpu.VMEM((3, 2, SIDE, span // 16, WIDE), BF16),
            pltpu.VMEM((SIDE, 2, span // 16, WIDE), BF16),
            pltpu.VMEM((3, 2, span // 16, WIDE), BF16),
            pltpu.VMEM((2, 2, wide // devices, WIDE), F32),
            pltpu.VMEM((2, wide // devices, WIDE), F32),
            pltpu.VMEM((span, span), BF16),
            pltpu.VMEM((2, 3, block, WIDE), BF16),
            pltpu.VMEM((2, LINE, 32, WIDE), BF16),
            pltpu.VMEM((LINE, 2, 32, WIDE), BF16),
            pltpu.VMEM((4, 8, 128), F32),
            pltpu.VMEM((4, 3, 8, 128), F32),
            sem((SIDE + 1,)),
            sem((LINE,)), sem((LINE,)),
            sem((2, 16)), sem((2, 16)),
            sem((2, 16)), sem((2, 16)),
            sem((3,)), sem((3,)),
            sem((3,)), sem((3,)),
            sem((3, SIDE)), sem((3, SIDE)),
            sem((SIDE, SIDE)), sem((SIDE, SIDE)),
            sem((2, SIDE)), sem((2, SIDE)),
            sem((2, SIDE)), sem((2, SIDE)),
            sem((2,)), sem((2,)),
            sem((2, 2)), sem((2, 2)),
            sem((SIDE,)), sem((SIDE,)),
            sem((2, SIDE)), sem((2, SIDE)),
            sem((3, 2, SIDE)), sem((3, 2, SIDE)),
            sem((3,)), sem((3,)),
            sem((3,)), sem((3,)),
            sem, sem,
            sem((2, 3)), sem((2, 3)),
            sem((LINE,)), sem((LINE,)),
            sem((4, 3)), sem((4, 3)),
        ],
        compiler_params=pltpu.CompilerParams(
            collective_id=0, has_side_effects=True, vmem_limit_bytes=64 * 1024 * 1024 - 65536
        ),
        name="sampled_softmax_step",
    )(
        hidden, w_query, adapter, item_emb, counts.reshape(1, items),
        positive.reshape(queries // 128, 128), loss_weight.reshape(queries // 128, 128),
    )
    gw, ga, loss = pl.pallas_call(
        functools.partial(finish_kernel, 1.0 / (queries * devices)),
        out_shape=(
            jax.ShapeDtypeStruct(gw.shape, F32),
            jax.ShapeDtypeStruct(ga.shape, F32),
            jax.ShapeDtypeStruct((1, 1), F32),
        ),
        in_specs=[vmem, vmem, vmem],
        out_specs=(vmem, vmem, vmem),
        name="finish",
    )(gw, ga, loss)
    return gw, ga, loss.reshape(())


def solution(mesh):
    placed = (P(AXES, None), P(AXES, None), P(), P(AXES, None), P(), P(AXES), P(AXES))
    return jax.shard_map(
        on_device,
        mesh=mesh,
        in_specs=placed,
        out_specs=(P(AXES, None), P(AXES, None), P()),
        check_vma=False,
    )
```
